32 devices in a mesh: groups: 2 (over y), layer: 4 (over z), latent: 4 (over x, core).
Axes of the slice: x: 2, y: 2, z: 4, core: 2. Of those that a mesh axis runs over, the one named last changes fastest.
Arguments:
- residuals: bfloat16 [4, 256, 2304], P('layer', 'groups'), parts along dimension 1, may hold values from -6 to 6
- targets: bfloat16 [4, 256, 2304], P('layer', 'groups'), parts along dimension 1, may hold values from -6 to 6
- enc_weight: bfloat16 [4, 2304, 8192], P('layer', None, 'latent'), may hold values from -0.125 to 0.125
- enc_bias: float32 [4, 8192], P('layer', 'latent'), may hold values from -2.5 to 2.5
- dec_weight: bfloat16 [4, 8192, 2304], P('layer', 'latent'), may hold values from -0.0625 to 0.0625
- out_gain: float32 [4, 2304], P('layer'), may hold values from 0.1 to 1.9
- block_list: int32 [4, 2, 24], P('layer', 'groups'), parts along dimension 1, may hold values from 0 to 63, as said below
- block_count: int32 [4, 2], P('layer', 'groups'), parts along dimension 1, may hold values from 1 to 24
Outputs:
- recon: bfloat16 [4, 256, 2304], P('layer', 'groups', 'latent'), parts along dimension 1
- code_grad: bfloat16 [4, 256, 8192], P('layer', 'groups', 'latent'), parts along dimension 1
- layer_loss: float32 [2, 4], P('groups', 'layer'), parts along dimension 0
The draws below stay inside these ranges and needn't reach their ends.
There are 2 independent parts, one for each index of `groups`. The reference program is written for one: setup_inputs(seed, part) draws one part's arguments, and reference() takes and returns one part's arrays. A program takes and returns all parts, laid end to end along the dimension named above; an argument that names none is the same for every part. Nothing has to cross between parts.
Inputs may be any that keep to these rules, and one draw needn't show every extreme that they name: `block_list`: within the first block_count entries of a row the blocks are distinct; later entries are unused.
All inputs are finite; a program needn't handle non-finite values.
Results may differ from the reference program's by a relative error of at most 0.0054.
Values may be sent and summed in bfloat16 or wider, within the bound.
No kernel may reach another device: no remote copies, remote signals or barrier semaphores. Data moves between devices by JAX's collectives and lax.ppermute only.
A program may use at most 128 MiB of HBM per device.

```python
import jax
import jax.numpy as jnp

D = 2304
LATENTS = 8192
BLOCK = 128
TILE = 128
KMAX = 24
TOK = 128
LAYERS = 4
TILES = 1
NBLOCK = 64


def draw_block_list(key, part):
    key = jax.random.fold_in(key, 11)
    row_keys = jax.random.split(key, LAYERS * TILES)
    rows = jax.vmap(lambda row_key: jax.random.permutation(row_key, NBLOCK)[:KMAX])(row_keys)
    return rows.reshape(LAYERS, TILES, KMAX).astype(jnp.int32)


def draw_block_count(key, part):
    key = jax.random.fold_in(key, 23)
    counts = jax.random.randint(key, (LAYERS, TILES), 1, KMAX + 1, dtype=jnp.int32)
    return counts.at[0, 0].set(KMAX)


def steps_of(rng, extent, cuts, low, high):
    def one(position, blocks):
        steps = jax.random.uniform(jax.random.fold_in(jax.random.fold_in(rng, 6), position), (blocks,), jnp.float32, low / len(cuts), high / len(cuts))
        return jnp.repeat(jnp.exp(steps), extent[position] // blocks).reshape((-1,) + (1,) * (len(extent) - position - 1))

    loudness = one(*cuts[0])
    for cut in cuts[1:]:
        loudness = loudness * one(*cut)
    return loudness


def gaussian(rng, extent, scale, most, pieces=(), kind=jnp.bfloat16):
    values = jax.random.normal(rng, extent, jnp.float32) * scale
    if len(pieces) > 0:
        values = steps_of(rng, extent, pieces, -0.22, 0.18) * values
    return jnp.clip(values, min=-most, max=most).astype(kind)


def setup_inputs(seed: int = 0, part: int = 0) -> dict:
    seeds = jax.random.split(jax.random.key(seed), 9)
    part_splits = jax.random.split(jax.random.fold_in(seeds[8], part), 9)
    return {
        "residuals": gaussian(part_splits[0], (LAYERS, TOK, D), 1.0, 6.0, ((0, 4),)),
        "targets": gaussian(part_splits[1], (LAYERS, TOK, D), 1.0, 6.0, ((0, 4),)),
        "enc_weight": gaussian(seeds[2], (LAYERS, D, LATENTS), D ** -0.5, 0.125, ((0, 4), (2, 4))),
        "enc_bias": gaussian(seeds[3], (LAYERS, LATENTS), 0.5, 2.5, ((0, 4), (1, 4)), jnp.float32),
        "dec_weight": gaussian(seeds[4], (LAYERS, LATENTS, D), LATENTS ** -0.5, 0.0625, ((0, 4), (1, 4))),
        "out_gain": jnp.clip(1.0 + 0.18 * jax.random.normal(seeds[5], (LAYERS, D), jnp.float32), 0.1, 1.9),
        "block_list": draw_block_list(jax.random.fold_in(jax.random.fold_in(seeds[8], part), 71), part),
        "block_count": draw_block_count(jax.random.fold_in(jax.random.fold_in(seeds[8], part), 71), part),
    }


def reference(residuals, targets, enc_weight, enc_bias, dec_weight, out_gain, block_list, block_count):
    nblock = LATENTS // BLOCK
    live_slots = jnp.arange(KMAX).astype(jnp.int32)[None, None, :] < block_count[:, :, None]
    block_ids = jnp.arange(nblock).astype(jnp.int32)
    block_mask = jnp.any((block_list[..., None] == block_ids) & live_slots[..., None], axis=2).astype(jnp.float32)

    def expand(layer):
        return jnp.repeat(jnp.repeat(block_mask[layer], TILE, axis=0), BLOCK, axis=1)

    partials = []
    for layer in range(LAYERS):
        pre_act = jnp.dot(residuals[layer], enc_weight[layer], preferred_element_type=jnp.float32) + enc_bias[layer][None, :]
        latent_codes = (expand(layer) * jnp.maximum(pre_act, 0.0)).astype(jnp.bfloat16)
        partials.append(jnp.dot(latent_codes, dec_weight[layer], preferred_element_type=jnp.float32))
    stacked = jnp.stack(partials)
    summed = jnp.cumsum(stacked, axis=0)
    fitted = out_gain[:, None, :] * summed
    recon = fitted.astype(jnp.bfloat16)
    error_term = fitted - targets.astype(jnp.float32)
    layer_loss = jnp.mean(error_term * error_term, axis=(1, 2))[None, :]
    backward = out_gain[:, None, :] * error_term
    suffix_part = jnp.flip(jnp.cumsum(jnp.flip(backward, 0), axis=0), 0)
    grad_in = suffix_part.astype(jnp.bfloat16)
    grads = []
    for layer in range(LAYERS):
        product = jnp.dot(grad_in[layer], dec_weight[layer].T, preferred_element_type=jnp.float32)
        grads.append((expand(layer) * product).astype(jnp.bfloat16))
    code_grad = jnp.stack(grads)
    return recon, code_grad, layer_loss
```

```python
import functools

import jax
import jax.numpy as jnp
from jax import lax
from jax.experimental import pallas as pl
from jax.experimental.pallas import tpu as pltpu
from jax.sharding import PartitionSpec as P

BLOCK = 128
PAIR = 2 * BLOCK
F32 = jnp.float32
BF16 = jnp.bfloat16


def encode_decode(list_ref, count_ref, x_ref, bias_ref, enc_ref, dec_ref, keep_ref, send_ref, dec_kept, ids_ref, enc_held, total, enc_sem, dec_sem):
    blocks = enc_ref.shape[1] // BLOCK
    where = lax.axis_index("latent")
    first = where * blocks
    slots = list_ref.shape[2]
    count = count_ref[0, 0]

    def copies(block, n):
        pair, half = lax.div(n, 2), lax.rem(n, 2) * BLOCK
        half = pl.multiple_of(half, BLOCK)
        start = pl.multiple_of(block * BLOCK, BLOCK)
        return (
            pltpu.make_async_copy(enc_ref.at[:, pl.ds(start, BLOCK)], enc_held.at[pair, :, pl.ds(half, BLOCK)], enc_sem.at[n]),
            pltpu.make_async_copy(dec_ref.at[pl.ds(start, BLOCK), :], dec_kept.at[pair, pl.ds(half, BLOCK), :], dec_sem.at[n]),
        )

    def look(slot, n):
        block = list_ref[0, 0, slot] - first
        live = (slot < count) & (block >= 0) & (block < blocks)

        @pl.when(live)
        def _():
            ids_ref[0, n] = block
            for copy in copies(block, n):
                copy.start()

        return n + live.astype(jnp.int32)

    live_count = lax.fori_loop(0, slots, look, jnp.int32(0))
    ids_ref[0, blocks] = live_count
    total[...] = jnp.zeros_like(total)
    pairs = lax.div(live_count + 1, 2)
    odd = lax.rem(live_count, 2) == 1

    @pl.when(odd)
    def _():
        dec_kept[pairs - 1, pl.ds(BLOCK, BLOCK), :] = jnp.zeros((BLOCK, dec_kept.shape[2]), BF16)
        ids_ref[0, live_count] = ids_ref[0, live_count - 1]

    def step(pair, carry):
        n = 2 * pair
        full = n + 1 < live_count
        one, two = ids_ref[0, n], ids_ref[0, n + 1]
        for copy in copies(one, n):
            copy.wait()

        @pl.when(full)
        def _():
            for copy in copies(two, n + 1):
                copy.wait()

        bias = jnp.concatenate(
            [bias_ref[:, pl.ds(pl.multiple_of(block * BLOCK, BLOCK), BLOCK)] for block in (one, two)], axis=1
        )
        pre_act = jnp.dot(x_ref[...], enc_held[pair], preferred_element_type=F32) + bias
        lane = lax.broadcasted_iota(jnp.int32, pre_act.shape, 1)
        used = (lane < BLOCK) | full
        codes = jnp.where(used, jnp.maximum(pre_act, 0.0), 0.0).astype(BF16)
        total[...] += jnp.dot(codes, dec_kept[pair], preferred_element_type=F32)
        return carry

    lax.fori_loop(0, pairs, step, 0)
    rows = keep_ref.shape[0]
    core = lax.rem(where, 2)
    keep_ref[...] = total[pl.ds(pl.multiple_of(core * rows, rows), rows), :]
    send_ref[...] = total[pl.ds(pl.multiple_of((1 - core) * rows, rows), rows), :].astype(BF16)


def code_gradient(ids_ref, own_ref, other_ref, dec_kept, out_ref, grad):
    blocks = out_ref.shape[1] // BLOCK
    rows = own_ref.shape[0]
    core = lax.rem(lax.axis_index("latent"), 2)
    grad[pl.ds(pl.multiple_of(core * rows, rows), rows), :] = own_ref[...]
    grad[pl.ds(pl.multiple_of((1 - core) * rows, rows), rows), :] = other_ref[...]
    out_ref[...] = jnp.zeros_like(out_ref)
    live_count = ids_ref[0, blocks]

    def step(pair, carry):
        n = 2 * pair
        product = lax.dot_general(
            grad[...], dec_kept[pair], (((1,), (1,)), ((), ())), preferred_element_type=F32
        ).astype(BF16)
        out_ref[:, pl.ds(pl.multiple_of(ids_ref[0, n] * BLOCK, BLOCK), BLOCK)] = product[:, :BLOCK]

        @pl.when(n + 1 < live_count)
        def _():
            out_ref[:, pl.ds(pl.multiple_of(ids_ref[0, n + 1] * BLOCK, BLOCK), BLOCK)] = product[:, BLOCK:]

        return carry

    lax.fori_loop(0, lax.div(live_count + 1, 2), step, 0)


def swap(value, axis, bit):
    size = lax.axis_size(axis)
    return lax.ppermute(value, axis, [(i, i ^ bit) for i in range(size)])


def swap_both(value, layer_bit, latent_bit):
    layers, latents = lax.axis_size("layer"), lax.axis_size("latent")
    pairs = [
        (l * latents + k, (l ^ layer_bit) * latents + (k ^ latent_bit)) for l in range(layers) for k in range(latents)
    ]
    return lax.ppermute(value, ("layer", "latent"), pairs)


def part(value, start, size, axis):
    return lax.dynamic_slice_in_dim(value, start, size, axis)


def local(residuals, targets, enc_weight, enc_bias, dec_weight, out_gain, block_list, block_count):
    tok_rows, model_width = residuals.shape[1:]
    local_latents = enc_weight.shape[2]
    blocks = local_latents // BLOCK
    pair_slots = (blocks + 1) // 2
    layers, latents = lax.axis_size("layer"), lax.axis_size("latent")
    layer, latent = lax.axis_index("layer"), lax.axis_index("latent")
    core = latent % 2
    rows = tok_rows // 2
    chips = latents // 2
    width = model_width // chips
    column = (latent // 2) * width

    gain = part(out_gain, column, width, 1)
    target = part(part(targets[0], core * rows, rows, 0), column, width, 1)
    square = gain * gain
    layer_bits = [1 << s for s in range((layers - 1).bit_length())]
    near_gain = swap(gain, "layer", 1)
    near_target = swap(target, "layer", 1)
    chip_bits = [1 << s for s in range((chips - 1).bit_length(), 0, -1)]

    vmem = pl.BlockSpec(memory_space=pltpu.VMEM)
    smem = pl.BlockSpec(memory_space=pltpu.SMEM)
    anyw = pl.BlockSpec(memory_space=pl.ANY)
    keep, send, dec_kept, ids = pl.pallas_call(
        encode_decode,
        out_shape=(
            jax.ShapeDtypeStruct((rows, model_width), F32),
            jax.ShapeDtypeStruct((rows, model_width), BF16),
            pltpu.VMEM((pair_slots, PAIR, model_width), BF16),
            jax.ShapeDtypeStruct((1, blocks + 1), jnp.int32),
        ),
        in_specs=[smem, smem, vmem, vmem, anyw, anyw],
        out_specs=(vmem, vmem, vmem, smem),
        scratch_shapes=[
            pltpu.VMEM((pair_slots, model_width, PAIR), BF16),
            pltpu.VMEM((tok_rows, model_width), F32),
            pltpu.SemaphoreType.DMA((blocks,)),
            pltpu.SemaphoreType.DMA((blocks,)),
        ],
        compiler_params=pltpu.CompilerParams(vmem_limit_bytes=48 << 20),
        name="encode_decode",
    )(block_list, block_count, residuals[0], enc_bias, enc_weight[0], dec_weight[0])

    held = keep + swap(send, "latent", 1).astype(F32)
    for bit in chip_bits[:-1]:
        half = held.shape[1] // 2
        upper = (latent & bit) != 0
        away = jnp.where(upper, held[:, :half], held[:, half:]).astype(BF16)
        mine = jnp.where(upper, held[:, half:], held[:, :half])
        held = mine + swap(away, "latent", bit).astype(F32)
    bit = chip_bits[-1]
    half = held.shape[1] // 2
    upper = (latent & bit) != 0
    away = jnp.where(upper, held[:, :half], held[:, half:]).astype(BF16)
    mine = jnp.where(upper, held[:, half:], held[:, :half])
    from_near = swap(mine.astype(BF16), "layer", 1)
    from_chip = swap(away, "latent", bit)
    from_both = swap_both(away, 1, bit)
    own = mine + from_chip.astype(F32)
    near = from_near.astype(F32) + from_both.astype(F32)

    low = (layer & 1) == 0
    near_square = near_gain * near_gain
    own_error = square * own - gain * target.astype(F32)
    near_error = near_square * near - near_gain * near_target.astype(F32)
    before = jnp.where(low, own, own + near)
    after = jnp.where(low, own_error + near_square * own + near_error, own_error + square * near)
    after_square = jnp.where(low, square + near_square, square)
    all_before = own + near
    all_after = own_error + near_error + jnp.where(low, near_square * own, square * near)
    all_square = square + near_square
    for step in layer_bits[1:]:
        low = (layer & step) == 0
        there_square = swap(all_square, "layer", step)
        if step == layer_bits[-1]:
            got = swap(jnp.where(low, all_before, all_after).astype(BF16), "layer", step).astype(F32)
            there_before = there_after = got
        else:
            there_before = swap(all_before.astype(BF16), "layer", step).astype(F32)
            there_after = swap(all_after.astype(BF16), "layer", step).astype(F32)
        before, after = (
            jnp.where(low, before, before + there_before),
            jnp.where(low, after + there_square * all_before + there_after, after + after_square * there_before),
        )
        after_square = jnp.where(low, after_square + there_square, after_square)
        all_before, all_after = (
            all_before + there_before,
            all_after + there_after + jnp.where(low, there_square * all_before, all_square * there_before),
        )
        all_square = all_square + there_square

    grad_in = after.astype(BF16)
    fitted = gain * before
    error_term = fitted - target.astype(F32)
    loss = jnp.sum(error_term * error_term).reshape(1, 1)

    for bit in reversed(chip_bits):
        upper = (latent & bit) != 0
        got = swap(grad_in, "latent", bit)
        grad_in = jnp.concatenate([jnp.where(upper, got, grad_in), jnp.where(upper, grad_in, got)], axis=1)
        loss = loss + swap(loss, "latent", bit)
    other_rows = swap(grad_in, "latent", 1)
    loss = (loss + swap(loss, "latent", 1)) / (tok_rows * model_width)

    recon = fitted.astype(BF16)
    columns = width // 2
    stay = part(recon, core * columns, columns, 1)
    got = swap(part(recon, (1 - core) * columns, columns, 1), "latent", 1)
    recon = jnp.concatenate([jnp.where(core == 0, stay, got), jnp.where(core == 0, got, stay)], axis=0)

    code_grad = pl.pallas_call(
        code_gradient,
        out_shape=jax.ShapeDtypeStruct((tok_rows, local_latents), BF16),
        in_specs=[smem, vmem, vmem, vmem],
        out_specs=vmem,
        scratch_shapes=[pltpu.VMEM((tok_rows, model_width), BF16)],
        compiler_params=pltpu.CompilerParams(vmem_limit_bytes=24 << 20),
        name="code_gradient",
    )(ids, grad_in, other_rows, pltpu.with_memory_space_constraint(dec_kept, pltpu.VMEM))
    return recon[None], code_grad[None], loss


def solution(mesh):
    placed = (
        P("layer", "groups", None),
        P("layer", "groups", None),
        P("layer", None, "latent"),
        P("layer", "latent"),
        P("layer", "latent", None),
        P("layer", None),
        P("layer", "groups", None),
        P("layer", "groups"),
    )
    return jax.shard_map(
        local,
        mesh=mesh,
        in_specs=placed,
        out_specs=(
            P("layer", "groups", "latent"),
            P("layer", "groups", "latent"),
            P("groups", "layer"),
        ),
        check_vma=False,
    )
```

```python
import functools

import jax
import jax.numpy as jnp
from jax import lax
from jax.experimental import pallas as pl
from jax.experimental.pallas import tpu as pltpu
from jax.sharding import PartitionSpec as P

BLOCK = 128
PAIR = 2 * BLOCK
KEPT_PAIRS = 1
F32 = jnp.float32
BF16 = jnp.bfloat16


def dec_copy(dec_ref, dec_kept, dec_more, sem, block, n, start):
    kept = dec_kept.shape[0]
    pair, half = lax.div(n, 2), pl.multiple_of(lax.rem(n, 2) * BLOCK, BLOCK)
    source = dec_ref.at[pl.ds(pl.multiple_of(block * BLOCK, BLOCK), BLOCK), :]

    def move(held, slot):
        copy = pltpu.make_async_copy(source, held.at[slot, pl.ds(half, BLOCK), :], sem.at[n])
        copy.start() if start else copy.wait()

    pl.when(pair < kept)(lambda: move(dec_kept, pair))
    pl.when(pair >= kept)(lambda: move(dec_more, pair - kept))


def encode_decode(list_ref, count_ref, x_any, bias_any, enc_ref, dec_ref, keep_ref, send_ref, dec_kept, ids_ref, x_ref, bias_ref, dec_more, enc_held, total, in_sem, enc_sem, dec_sem):
    loads = [pltpu.make_async_copy(x_any, x_ref, in_sem.at[0]), pltpu.make_async_copy(bias_any, bias_ref, in_sem.at[1])]
    for load in loads:
        load.start()
    blocks = enc_ref.shape[1] // BLOCK
    where = lax.axis_index("latent")
    first = where * blocks
    slots = list_ref.shape[2]
    count = count_ref[0, 0]

    kept = dec_kept.shape[0]

    def enc_copy(block, n):
        half = pl.multiple_of(lax.rem(n, 2) * BLOCK, BLOCK)
        return pltpu.make_async_copy(
            enc_ref.at[:, pl.ds(pl.multiple_of(block * BLOCK, BLOCK), BLOCK)],
            enc_held.at[lax.div(n, 2), :, pl.ds(half, BLOCK)],
            enc_sem.at[n],
        )

    def look(slot, n):
        block = list_ref[0, 0, slot] - first
        live = (slot < count) & (block >= 0) & (block < blocks)

        @pl.when(live)
        def _():
            ids_ref[0, n] = block
            enc_copy(block, n).start()
            dec_copy(dec_ref, dec_kept, dec_more, dec_sem, block, n, True)

        return n + live.astype(jnp.int32)

    live_count = lax.fori_loop(0, slots, look, jnp.int32(0))
    ids_ref[0, blocks] = live_count
    total[...] = jnp.zeros_like(total)
    pairs = lax.div(live_count + 1, 2)
    odd = lax.rem(live_count, 2) == 1

    @pl.when(odd)
    def _():
        zeros = jnp.zeros((BLOCK, dec_kept.shape[2]), BF16)

        @pl.when(pairs <= kept)
        def _():
            dec_kept[pairs - 1, pl.ds(BLOCK, BLOCK), :] = zeros

        @pl.when(pairs > kept)
        def _():
            dec_more[pairs - 1 - kept, pl.ds(BLOCK, BLOCK), :] = zeros

        ids_ref[0, live_count] = ids_ref[0, live_count - 1]

    for load in loads:
        load.wait()

    def step(held, offset, pair, carry):
        n = 2 * pair
        full = n + 1 < live_count
        one, two = ids_ref[0, n], ids_ref[0, n + 1]
        enc_copy(one, n).wait()
        dec_copy(dec_ref, dec_kept, dec_more, dec_sem, one, n, False)

        @pl.when(full)
        def _():
            enc_copy(two, n + 1).wait()
            dec_copy(dec_ref, dec_kept, dec_more, dec_sem, two, n + 1, False)

        bias = jnp.concatenate(
            [bias_ref[:, pl.ds(pl.multiple_of(block * BLOCK, BLOCK), BLOCK)] for block in (one, two)], axis=1
        )
        pre_act = jnp.dot(x_ref[...], enc_held[pair], preferred_element_type=F32) + bias
        lane = lax.broadcasted_iota(jnp.int32, pre_act.shape, 1)
        used = (lane < BLOCK) | full
        codes = jnp.where(used, jnp.maximum(pre_act, 0.0), 0.0).astype(BF16)
        total[...] += jnp.dot(codes, held[pair - offset], preferred_element_type=F32)
        return carry

    lax.fori_loop(0, jnp.minimum(pairs, kept), functools.partial(step, dec_kept, 0), 0)
    lax.fori_loop(kept, pairs, functools.partial(step, dec_more, kept), 0)
    rows = keep_ref.shape[0]
    core = lax.rem(where, 2)
    keep_ref[...] = total[pl.ds(pl.multiple_of(core * rows, rows), rows), :]
    send_ref[...] = total[pl.ds(pl.multiple_of((1 - core) * rows, rows), rows), :].astype(BF16)


def code_gradient(ids_ref, own_ref, other_ref, loss_ref, chip_loss_ref, dec_kept, dec_ref, out_ref, mean_ref, grad, dec_more, dec_sem):
    blocks = out_ref.shape[1] // BLOCK
    kept = dec_kept.shape[0]
    rows = own_ref.shape[0]
    live_count = ids_ref[0, blocks]

    def fetch(n, carry):
        dec_copy(dec_ref, dec_kept, dec_more, dec_sem, ids_ref[0, n], n, True)
        return carry

    lax.fori_loop(2 * kept, live_count, fetch, 0)
    core = lax.rem(lax.axis_index("latent"), 2)
    grad[pl.ds(pl.multiple_of(core * rows, rows), rows), :] = own_ref[...]
    grad[pl.ds(pl.multiple_of((1 - core) * rows, rows), rows), :] = other_ref[...]
    out_ref[...] = jnp.zeros_like(out_ref)
    both = loss_ref[...] + chip_loss_ref[...]
    mean_ref[...] = jnp.sum(both, axis=1, keepdims=True) / (2 * rows * own_ref.shape[1])

    def step(held, offset, pair, carry):
        n = 2 * pair
        full = n + 1 < live_count

        if offset:
            dec_copy(dec_ref, dec_kept, dec_more, dec_sem, ids_ref[0, n], n, False)

            @pl.when(full)
            def _():
                dec_copy(dec_ref, dec_kept, dec_more, dec_sem, ids_ref[0, n + 1], n + 1, False)

        product = lax.dot_general(
            grad[...], held[pair - offset], (((1,), (1,)), ((), ())), preferred_element_type=F32
        ).astype(BF16)
        out_ref[:, pl.ds(pl.multiple_of(ids_ref[0, n] * BLOCK, BLOCK), BLOCK)] = product[:, :BLOCK]

        @pl.when(full)
        def _():
            out_ref[:, pl.ds(pl.multiple_of(ids_ref[0, n + 1] * BLOCK, BLOCK), BLOCK)] = product[:, BLOCK:]

        return carry

    pairs = lax.div(live_count + 1, 2)
    lax.fori_loop(0, jnp.minimum(pairs, kept), functools.partial(step, dec_kept, 0), 0)
    lax.fori_loop(kept, pairs, functools.partial(step, dec_more, kept), 0)


def swap(value, axis, bit):
    size = lax.axis_size(axis)
    return lax.ppermute(value, axis, [(i, i ^ bit) for i in range(size)])


def swap_both(value, layer_bit, latent_bit):
    layers, latents = lax.axis_size("layer"), lax.axis_size("latent")
    pairs = [
        (l * latents + k, (l ^ layer_bit) * latents + (k ^ latent_bit)) for l in range(layers) for k in range(latents)
    ]
    return lax.ppermute(value, ("layer", "latent"), pairs)


def part(value, start, size, axis):
    return lax.dynamic_slice_in_dim(value, start, size, axis)


def local(residuals, targets, enc_weight, enc_bias, dec_weight, out_gain, block_list, block_count):
    tok_rows, model_width = residuals.shape[1:]
    local_latents = enc_weight.shape[2]
    blocks = local_latents // BLOCK
    pair_slots = (blocks + 1) // 2
    kept = min(KEPT_PAIRS, pair_slots)
    more = max(pair_slots - kept, 1)
    layers, latents = lax.axis_size("layer"), lax.axis_size("latent")
    layer, latent = lax.axis_index("layer"), lax.axis_index("latent")
    core = latent % 2
    rows = tok_rows // 2
    chips = latents // 2
    width = model_width // chips
    column = (latent // 2) * width

    gain = part(out_gain, column, width, 1)
    target = part(part(targets[0], core * rows, rows, 0), column, width, 1)
    square = gain * gain
    layer_bits = [1 << s for s in range((layers - 1).bit_length())]
    near_gain = swap(gain, "layer", 1)
    near_target = swap(target, "layer", 1)
    chip_bits = [1 << s for s in range((chips - 1).bit_length(), 0, -1)]

    dec_hbm = pltpu.with_memory_space_constraint(dec_weight[0], pltpu.HBM)
    vmem = pl.BlockSpec(memory_space=pltpu.VMEM)
    smem = pl.BlockSpec(memory_space=pltpu.SMEM)
    anyw = pl.BlockSpec(memory_space=pl.ANY)
    keep, send, dec_kept, ids = pl.pallas_call(
        encode_decode,
        out_shape=(
            pltpu.VMEM((rows, model_width), F32),
            pltpu.VMEM((rows, model_width), BF16),
            pltpu.VMEM((kept, PAIR, model_width), BF16),
            pltpu.SMEM((1, blocks + 1), jnp.int32),
        ),
        in_specs=[smem, smem, anyw, anyw, anyw, anyw],
        out_specs=(vmem, vmem, vmem, smem),
        scratch_shapes=[
            pltpu.VMEM((tok_rows, model_width), BF16),
            pltpu.VMEM((1, local_latents), F32),
            pltpu.VMEM((more, PAIR, model_width), BF16),
            pltpu.VMEM((pair_slots, model_width, PAIR), BF16),
            pltpu.VMEM((tok_rows, model_width), F32),
            pltpu.SemaphoreType.DMA((2,)),
            pltpu.SemaphoreType.DMA((blocks,)),
            pltpu.SemaphoreType.DMA((blocks,)),
        ],
        compiler_params=pltpu.CompilerParams(vmem_limit_bytes=32 << 20),
        name="encode_decode",
    )(block_list, block_count, *[pltpu.with_memory_space_constraint(a, pltpu.HBM) for a in (residuals[0], enc_bias, enc_weight[0])], dec_hbm)

    held = keep + swap(send, "latent", 1).astype(F32)
    for bit in chip_bits[:-1]:
        half = held.shape[1] // 2
        upper = (latent & bit) != 0
        away = jnp.where(upper, held[:, :half], held[:, half:]).astype(BF16)
        mine = jnp.where(upper, held[:, half:], held[:, :half])
        held = mine + swap(away, "latent", bit).astype(F32)
    bit = chip_bits[-1]
    half = held.shape[1] // 2
    upper = (latent & bit) != 0
    away = jnp.where(upper, held[:, :half], held[:, half:]).astype(BF16)
    mine = jnp.where(upper, held[:, half:], held[:, :half])
    from_near = swap(mine.astype(BF16), "layer", 1)
    from_chip = swap(away, "latent", bit)
    from_both = swap_both(away, 1, bit)
    own = mine + from_chip.astype(F32)
    near = from_near.astype(F32) + from_both.astype(F32)

    low = (layer & 1) == 0
    near_square = near_gain * near_gain
    own_error = square * own - gain * target.astype(F32)
    near_error = near_square * near - near_gain * near_target.astype(F32)
    before = jnp.where(low, own, own + near)
    after = jnp.where(low, own_error + near_square * own + near_error, own_error + square * near)
    after_square = jnp.where(low, square + near_square, square)
    all_before = own + near
    all_after = own_error + near_error + jnp.where(low, near_square * own, square * near)
    all_square = square + near_square
    for step in layer_bits[1:]:
        low = (layer & step) == 0
        there_square = swap(all_square, "layer", step)
        if step == layer_bits[-1]:
            got = swap(jnp.where(low, all_before, all_after).astype(BF16), "layer", step).astype(F32)
            there_before = there_after = got
        else:
            there_before = swap(all_before.astype(BF16), "layer", step).astype(F32)
            there_after = swap(all_after.astype(BF16), "layer", step).astype(F32)
        before, after = (
            jnp.where(low, before, before + there_before),
            jnp.where(low, after + there_square * all_before + there_after, after + after_square * there_before),
        )
        after_square = jnp.where(low, after_square + there_square, after_square)
        all_before, all_after = (
            all_before + there_before,
            all_after + there_after + jnp.where(low, there_square * all_before, all_square * there_before),
        )
        all_square = all_square + there_square

    grad_in = after.astype(BF16)
    before, grad_in = lax.optimization_barrier((before, grad_in))
    fitted = gain * before
    error_term = fitted - target.astype(F32)
    loss = jnp.sum(error_term * error_term, axis=0, keepdims=True)
    recon = fitted.astype(BF16)

    other_loss = swap(loss, "latent", 1)
    loss = loss + other_loss
    chip_loss = jnp.zeros_like(loss)
    for bit in reversed(chip_bits):
        upper = (latent & bit) != 0
        got = swap(grad_in, "latent", bit)
        if bit != chip_bits[0]:
            loss = loss + swap(loss, "latent", bit)
        else:
            chip_loss = swap(loss, "latent", bit)
        grad_in = jnp.concatenate([jnp.where(upper, got, grad_in), jnp.where(upper, grad_in, got)], axis=1)
    other_rows = swap(grad_in, "latent", 1)

    columns = width // 2
    stay = part(recon, core * columns, columns, 1)
    got = swap(part(recon, (1 - core) * columns, columns, 1), "latent", 1)
    recon = jnp.concatenate([jnp.where(core == 0, stay, got), jnp.where(core == 0, got, stay)], axis=0)

    code_grad, loss = pl.pallas_call(
        code_gradient,
        out_shape=(
            jax.ShapeDtypeStruct((tok_rows, local_latents), BF16),
            jax.ShapeDtypeStruct((1, 1), F32),
        ),
        in_specs=[smem, vmem, vmem, vmem, vmem, vmem, anyw],
        out_specs=(vmem, vmem),
        scratch_shapes=[
            pltpu.VMEM((tok_rows, model_width), BF16),
            pltpu.VMEM((more, PAIR, model_width), BF16),
            pltpu.SemaphoreType.DMA((blocks,)),
        ],
        compiler_params=pltpu.CompilerParams(vmem_limit_bytes=16 << 20),
        name="code_gradient",
    )(ids, grad_in, other_rows, loss, chip_loss, pltpu.with_memory_space_constraint(dec_kept, pltpu.VMEM), dec_hbm)
    return recon[None], code_grad[None], loss


def solution(mesh):
    placed = (
        P("layer", "groups", None),
        P("layer", "groups", None),
        P("layer", None, "latent"),
        P("layer", "latent"),
        P("layer", "latent", None),
        P("layer", None),
        P("layer", "groups", None),
        P("layer", "groups"),
    )
    return jax.shard_map(
        local,
        mesh=mesh,
        in_specs=placed,
        out_specs=(
            P("layer", "groups", "latent"),
            P("layer", "groups", "latent"),
            P("groups", "layer"),
        ),
        check_vma=False,
    )
```

```python
import functools

import jax
import jax.numpy as jnp
from jax import lax
from jax.experimental import pallas as pl
from jax.experimental.pallas import tpu as pltpu
from jax.sharding import PartitionSpec as P

BLOCK = 128
PAIR = 2 * BLOCK
KEPT_PAIRS = 3
F32 = jnp.float32
BF16 = jnp.bfloat16


def encode_decode(
    list_any, count_ref, x_any, bias_any, enc_ref, dec_ref, keep_ref, send_ref, ids_ref,
    list_ref, x_ref, bias_ref, enc_held, dec_held, codes, total, in_sem, enc_sem, dec_sem,
):
    blocks = enc_ref.shape[1] // BLOCK
    list_load = pltpu.make_async_copy(list_any, list_ref, in_sem.at[0])
    list_load.start()
    loads = [pltpu.make_async_copy(x_any, x_ref, in_sem.at[1]), pltpu.make_async_copy(bias_any, bias_ref, in_sem.at[2])]
    for load in loads:
        load.start()
    where = lax.axis_index("latent")
    first = where * blocks
    slots = list_ref.shape[2]
    count = count_ref[0, 0]
    total[...] = jnp.zeros_like(total)

    def copies(block, n):
        pair, half = lax.div(n, 2), pl.multiple_of(lax.rem(n, 2) * BLOCK, BLOCK)
        source = pl.ds(pl.multiple_of(block * BLOCK, BLOCK), BLOCK)
        return (
            pltpu.make_async_copy(enc_ref.at[:, source], enc_held.at[pair, :, pl.ds(half, BLOCK)], enc_sem.at[n]),
            pltpu.make_async_copy(dec_ref.at[source, :], dec_held.at[pair, pl.ds(half, BLOCK), :], dec_sem.at[n]),
        )

    def look(slot, n):
        block = list_ref[0, 0, slot] - first
        live = (slot < count) & (block >= 0) & (block < blocks)

        @pl.when(live)
        def _():
            ids_ref[0, n] = block
            for copy in copies(block, n):
                copy.start()

        return n + live.astype(jnp.int32)

    list_load.wait()
    live_count = lax.fori_loop(0, slots, look, jnp.int32(0))
    ids_ref[0, blocks] = live_count
    pairs = lax.div(live_count + 1, 2)

    @pl.when(lax.rem(live_count, 2) == 1)
    def _():
        dec_held[pairs - 1, pl.ds(BLOCK, BLOCK), :] = jnp.zeros((BLOCK, dec_held.shape[2]), BF16)
        ids_ref[0, live_count] = ids_ref[0, live_count - 1]

    for load in loads:
        load.wait()

    def arrive(pair, which):
        n = 2 * pair
        copies(ids_ref[0, n], n)[which].wait()

        @pl.when(n + 1 < live_count)
        def _():
            copies(ids_ref[0, n + 1], n + 1)[which].wait()

    def encode(pair):
        n = 2 * pair
        bias = jnp.concatenate(
            [bias_ref[:, pl.ds(pl.multiple_of(ids_ref[0, i] * BLOCK, BLOCK), BLOCK)] for i in (n, n + 1)], axis=1
        )
        pre_act = jnp.dot(x_ref[...], enc_held[pair], preferred_element_type=F32) + bias
        lane = lax.broadcasted_iota(jnp.int32, pre_act.shape, 1)
        used = (lane < BLOCK) | (n + 1 < live_count)
        codes[lax.rem(pair, 2)] = jnp.where(used, jnp.maximum(pre_act, 0.0), 0.0).astype(BF16)

    def decode(pair):
        total[...] += jnp.dot(codes[lax.rem(pair, 2)], dec_held[pair], preferred_element_type=F32)

    def step(pair, carry):
        arrive(pair, 0)
        arrive(pair - 1, 1)
        encode(pair)
        decode(pair - 1)
        return carry

    @pl.when(pairs > 0)
    def _():
        arrive(0, 0)
        encode(0)
        lax.fori_loop(1, pairs, step, 0)
        arrive(pairs - 1, 1)
        decode(pairs - 1)

    rows = keep_ref.shape[0]
    core = lax.rem(where, 2)
    keep_ref[...] = total[pl.ds(pl.multiple_of(core * rows, rows), rows), :]
    send_ref[...] = total[pl.ds(pl.multiple_of((1 - core) * rows, rows), rows), :].astype(BF16)


def finish(
    got_ref, before_ref, after_ref, all_ref, there_square_ref, after_square_ref, gain_ref, target_ref,
    message_ref, stay_ref, send_ref,
):
    got = got_ref[...].astype(F32)
    width = got.shape[1]
    low = (lax.axis_index("layer") & (lax.axis_size("layer") // 2)) == 0
    fitted = gain_ref[...] * jnp.where(low, before_ref[...], before_ref[...] + got)
    error_term = fitted - target_ref[...].astype(F32)
    squares = error_term * error_term
    added = functools.reduce(add_terms, [squares[:, i : i + BLOCK] for i in range(0, width - BLOCK + 1, BLOCK)])
    rest = width % BLOCK
    if rest:
        zeros = jnp.zeros((squares.shape[0], BLOCK - rest), F32)
        added = added + jnp.concatenate([squares[:, width - rest :], zeros], axis=1)
    entering = jnp.where(low, there_square_ref[...] * all_ref[...] + got, after_square_ref[...] * got)
    message_ref[:, :width] = (after_ref[...] + entering).astype(BF16)
    message_ref[:, width:] = added.astype(BF16)
    left, right = fitted[:, : width // 2].astype(BF16), fitted[:, width // 2 :].astype(BF16)
    first = (lax.axis_index("latent") & 1) == 0
    stay_ref[...] = jnp.where(first, left, right)
    send_ref[...] = jnp.where(first, right, left)


def add_terms(one, two):
    return one + two


def rows_of(dec_ref, block, half):
    cut = dec_ref.shape[1] // 2
    return dec_ref.at[pl.ds(pl.multiple_of(block * BLOCK, BLOCK), BLOCK), pl.ds(pl.multiple_of(half * cut, cut), cut)]


def place_of(n):
    return lax.div(n, 2), pl.ds(pl.multiple_of(lax.rem(n, 2) * BLOCK, BLOCK), BLOCK)


def by_core(core, mine, theirs, held):
    rows = mine.shape[0]
    held[pl.ds(pl.multiple_of(core * rows, rows), rows), :] = mine
    held[pl.ds(pl.multiple_of((1 - core) * rows, rows), rows), :] = theirs


def times_rows(grad, rows):
    return lax.dot_general(grad, rows, (((1,), (1,)), ((), ())), preferred_element_type=F32)


def near_gradient(top, ids_ref, own_ref, near_ref, dec_ref, part_ref, far_kept, grad, dec_near, near_sem, far_sem):
    blocks = near_sem.shape[0]
    kept, _, cut = far_kept.shape
    latent = lax.axis_index("latent")
    here = lax.div(latent & top, top)
    live_count = ids_ref[0, blocks]
    far_count = jnp.minimum(live_count, 2 * kept)

    def near_copy(n):
        pair, place = place_of(n)
        return pltpu.make_async_copy(rows_of(dec_ref, ids_ref[0, n], here), dec_near.at[pair, place, :], near_sem.at[n])

    def far_copy(n):
        pair, place = place_of(n)
        return pltpu.make_async_copy(rows_of(dec_ref, ids_ref[0, n], 1 - here), far_kept.at[pair, place, :], far_sem.at[n])

    lax.fori_loop(0, live_count, lambda n, c: (near_copy(n).start(), c)[1], 0)
    lax.fori_loop(0, far_count, lambda n, c: (far_copy(n).start(), c)[1], 0)
    by_core(latent & 1, own_ref[:, :cut], near_ref[:, :cut], grad)

    def step(pair, carry):
        n = 2 * pair
        near_copy(n).wait()
        pl.when(n + 1 < live_count)(lambda: near_copy(n + 1).wait())
        part_ref[pair] = times_rows(grad[...], dec_near[pair])
        return carry

    lax.fori_loop(0, lax.div(live_count + 1, 2), step, 0)
    lax.fori_loop(0, far_count, lambda n, c: (far_copy(n).wait(), c)[1], 0)


def code_gradient(
    top, ids_ref, own_ref, near_ref, got_ref, far_ref, stay_ref, part_ref, far_kept, dec_ref,
    out_ref, recon_ref, mean_ref, grad, fitted, dec_far, far_sem,
):
    blocks = far_sem.shape[0]
    kept, _, cut = far_kept.shape
    latent = lax.axis_index("latent")
    there = 1 - lax.div(latent & top, top)
    core = latent & 1
    live_count = ids_ref[0, blocks]
    pairs = lax.div(live_count + 1, 2)

    def far_copy(n):
        pair, place = place_of(n - 2 * kept)
        return pltpu.make_async_copy(rows_of(dec_ref, ids_ref[0, n], there), dec_far.at[pair, place, :], far_sem.at[n])

    lax.fori_loop(2 * kept, live_count, lambda n, c: (far_copy(n).start(), c)[1], 0)
    by_core(core, got_ref[:, :cut], far_ref[:, :cut], grad)
    out_ref[...] = jnp.zeros_like(out_ref)

    def store(pair, product):
        n = 2 * pair
        out_ref[:, pl.ds(pl.multiple_of(ids_ref[0, n] * BLOCK, BLOCK), BLOCK)] = product[:, :BLOCK]

        @pl.when(n + 1 < live_count)
        def _():
            out_ref[:, pl.ds(pl.multiple_of(ids_ref[0, n + 1] * BLOCK, BLOCK), BLOCK)] = product[:, BLOCK:]

    def step(pair, carry):
        store(pair, (part_ref[pair] + times_rows(grad[...], far_kept[pair])).astype(BF16))
        return carry

    def fetched(pair, carry):
        n = 2 * pair
        far_copy(n).wait()
        pl.when(n + 1 < live_count)(lambda: far_copy(n + 1).wait())
        store(pair, (part_ref[pair] + times_rows(grad[...], dec_far[pair - kept])).astype(BF16))
        return carry

    lax.fori_loop(0, jnp.minimum(pairs, kept), step, 0)
    lax.fori_loop(kept, pairs, fetched, 0)
    columns = stay_ref.shape[1]
    by_core(core, stay_ref[...].astype(F32), near_ref[:, cut + BLOCK :].astype(F32), fitted)
    recon_ref[...] = jnp.transpose(fitted[...]).astype(BF16)
    squares = sum(ref[:, cut : cut + BLOCK].astype(F32) for ref in (own_ref, near_ref, got_ref, far_ref))
    total = jnp.sum(jnp.sum(squares, axis=0, keepdims=True), axis=1, keepdims=True)
    mean_ref[...] = total / (grad.shape[0] * 2 * cut)


def swap(value, axis, bit):
    size = lax.axis_size(axis)
    return lax.ppermute(value, axis, [(i, i ^ bit) for i in range(size)])


def in_hbm(value):
    return pltpu.with_memory_space_constraint(value, pltpu.HBM)


def part(value, start, size, axis):
    return lax.dynamic_slice_in_dim(value, start, size, axis)


def local(residuals, targets, enc_weight, enc_bias, dec_weight, out_gain, block_list, block_count):
    tok_rows, model_width = residuals.shape[1:]
    local_latents = enc_weight.shape[2]
    blocks = local_latents // BLOCK
    pair_slots = (blocks + 1) // 2
    kept = min(KEPT_PAIRS, pair_slots)
    more = max(pair_slots - kept, 1)
    layers, latents = lax.axis_size("layer"), lax.axis_size("latent")
    layer, latent = lax.axis_index("layer"), lax.axis_index("latent")
    core = latent % 2
    rows = tok_rows // 2
    chips = latents // 2
    width = model_width // chips
    column = (latent // 2) * width

    gain = part(out_gain, column, width, 1)
    target = part(part(targets[0], core * rows, rows, 0), column, width, 1)
    terms, left = [], gain
    for _ in range(3):
        terms.append(lax.reduce_precision(left, 8, 7))
        left = left - terms[-1]
    beside = jnp.concatenate([target, *[term.astype(BF16) for term in terms], jnp.zeros((13, width), BF16)], axis=0)
    layer_bits = [1 << s for s in range((layers - 1).bit_length())]
    chip_bits = [1 << s for s in range((chips - 1).bit_length(), 0, -1)]

    dec_hbm = in_hbm(dec_weight[0])
    vmem = pl.BlockSpec(memory_space=pltpu.VMEM)
    smem = pl.BlockSpec(memory_space=pltpu.SMEM)
    anyw = pl.BlockSpec(memory_space=pl.ANY)
    keep, send, ids = pl.pallas_call(
        encode_decode,
        out_shape=(
            pltpu.VMEM((rows, model_width), F32),
            pltpu.VMEM((rows, model_width), BF16),
            pltpu.SMEM((1, blocks + 1), jnp.int32),
        ),
        in_specs=[anyw, smem, anyw, anyw, anyw, anyw],
        out_specs=(vmem, vmem, smem),
        scratch_shapes=[
            pltpu.SMEM(block_list.shape, jnp.int32),
            pltpu.VMEM((tok_rows, model_width), BF16),
            pltpu.VMEM((1, local_latents), F32),
            pltpu.VMEM((pair_slots, model_width, PAIR), BF16),
            pltpu.VMEM((pair_slots, PAIR, model_width), BF16),
            pltpu.VMEM((2, tok_rows, PAIR), BF16),
            pltpu.VMEM((tok_rows, model_width), F32),
            pltpu.SemaphoreType.DMA((3,)),
            pltpu.SemaphoreType.DMA((blocks,)),
            pltpu.SemaphoreType.DMA((blocks,)),
        ],
        compiler_params=pltpu.CompilerParams(vmem_limit_bytes=32 << 20),
        name="encode_decode",
    )(in_hbm(block_list), block_count, in_hbm(residuals[0]), in_hbm(enc_bias), in_hbm(enc_weight[0]), dec_hbm)

    held = keep + swap(send, "latent", 1).astype(F32)
    for bit in chip_bits:
        half = held.shape[1] // 2
        upper = (latent & bit) != 0
        away = jnp.where(upper, held[:, :half], held[:, half:]).astype(BF16)
        mine = jnp.where(upper, held[:, half:], held[:, :half])
        if bit == chip_bits[-1]:
            away, beside = lax.optimization_barrier((away, beside))
            beside = swap(beside, "layer", 1)
        held = mine + swap(away, "latent", bit).astype(F32)
    own = held
    near = swap(own.astype(BF16), "layer", 1).astype(F32)
    near_target = beside[:rows]
    near_gain = sum(beside[rows + i : rows + i + 1].astype(F32) for i in range(3))
    square = gain * gain
    near_square = near_gain * near_gain
    all_square = square + near_square

    low = (layer & 1) == 0
    own_error = square * own - gain * target.astype(F32)
    near_error = near_square * near - near_gain * near_target.astype(F32)
    before = jnp.where(low, own, own + near)
    after = jnp.where(low, own_error + near_square * own + near_error, own_error + square * near)
    after_square = jnp.where(low, square + near_square, square)
    all_before = own + near
    all_after = own_error + near_error + jnp.where(low, near_square * own, square * near)
    for step in layer_bits[1:]:
        low = (layer & step) == 0
        there_square = swap(all_square, "layer", step)
        if step == layer_bits[-1]:
            got = swap(jnp.where(low, all_before, all_after).astype(BF16), "layer", step)
            break
        there_before = swap(all_before.astype(BF16), "layer", step).astype(F32)
        there_after = swap(all_after.astype(BF16), "layer", step).astype(F32)
        before, after = (
            jnp.where(low, before, before + there_before),
            jnp.where(low, after + there_square * all_before + there_after, after + after_square * there_before),
        )
        after_square = jnp.where(low, after_square + there_square, after_square)
        all_before, all_after = (
            all_before + there_before,
            all_after + there_after + jnp.where(low, there_square * all_before, all_square * there_before),
        )
        all_square = all_square + there_square

    columns = width // 2
    message, stay, send = pl.pallas_call(
        finish,
        out_shape=(
            pltpu.VMEM((rows, width + BLOCK), BF16),
            pltpu.VMEM((rows, columns), BF16),
            pltpu.VMEM((rows, columns), BF16),
        ),
        in_specs=[vmem] * 8,
        out_specs=(vmem, vmem, vmem),
        compiler_params=pltpu.CompilerParams(vmem_limit_bytes=16 << 20),
        name="finish",
    )(got, before, after, all_before, there_square, after_square, gain, target)

    for bit in reversed(chip_bits[1:]):
        upper = (latent & bit) != 0
        got = swap(message, "latent", bit)
        cut = message.shape[1] - BLOCK
        here, there = message[:, :cut], got[:, :cut]
        squares = (message[:, cut:].astype(F32) + got[:, cut:].astype(F32)).astype(BF16)
        message = jnp.concatenate([jnp.where(upper, there, here), jnp.where(upper, here, there), squares], axis=1)
    top, cut = chip_bits[0], model_width // 2
    got = swap(message, "latent", top)
    near = swap(jnp.concatenate([message, send], axis=1), "latent", 1)
    near_part, far_kept = pl.pallas_call(
        functools.partial(near_gradient, top),
        out_shape=(pltpu.VMEM((pair_slots, tok_rows, PAIR), F32), pltpu.VMEM((kept, PAIR, cut), BF16)),
        in_specs=[smem, vmem, vmem, anyw],
        out_specs=(vmem, vmem),
        scratch_shapes=[
            pltpu.VMEM((tok_rows, cut), BF16),
            pltpu.VMEM((pair_slots, PAIR, cut), BF16),
            pltpu.SemaphoreType.DMA((blocks,)),
            pltpu.SemaphoreType.DMA((blocks,)),
        ],
        compiler_params=pltpu.CompilerParams(vmem_limit_bytes=24 << 20),
        cost_estimate=pl.CostEstimate(flops=2 * tok_rows * cut * local_latents, bytes_accessed=2 * local_latents * model_width, transcendentals=0),
        name="near_gradient",
    )(ids, message, near, dec_hbm)
    got, near_part = lax.optimization_barrier((got, near_part))
    far = swap(got, "latent", 1)

    code_grad, recon, loss = pl.pallas_call(
        functools.partial(code_gradient, top),
        out_shape=(
            jax.ShapeDtypeStruct((tok_rows, local_latents), BF16),
            jax.ShapeDtypeStruct((columns, tok_rows), BF16),
            jax.ShapeDtypeStruct((1, 1), F32),
        ),
        in_specs=[smem] + [vmem] * 7 + [anyw],
        out_specs=(vmem, vmem, vmem),
        scratch_shapes=[
            pltpu.VMEM((tok_rows, cut), BF16),
            pltpu.VMEM((tok_rows, columns), F32),
            pltpu.VMEM((more, PAIR, cut), BF16),
            pltpu.SemaphoreType.DMA((blocks,)),
        ],
        compiler_params=pltpu.CompilerParams(vmem_limit_bytes=16 << 20),
        name="code_gradient",
    )(ids, message, near, got, far, stay, *[pltpu.with_memory_space_constraint(a, pltpu.VMEM) for a in (near_part, far_kept)], dec_hbm)
    return recon.T[None], code_grad[None], loss


def solution(mesh):
    placed = (
        P("layer", "groups", None),
        P("layer", "groups", None),
        P("layer", None, "latent"),
        P("layer", "latent"),
        P("layer", "latent", None),
        P("layer", None),
        P("layer", "groups", None),
        P("layer", "groups"),
    )
    return jax.shard_map(
        local,
        mesh=mesh,
        in_specs=placed,
        out_specs=(
            P("layer", "groups", "latent"),
            P("layer", "groups", "latent"),
            P("groups", "layer"),
        ),
        check_vma=False,
    )
```

```python
import functools

import jax
import jax.numpy as jnp
from jax import lax
from jax.experimental import pallas as pl
from jax.experimental.pallas import tpu as pltpu
from jax.sharding import PartitionSpec as P

BLOCK = 128
PAIR = 2 * BLOCK
KEPT_PAIRS = 3
F32 = jnp.float32
BF16 = jnp.bfloat16


def encode_decode(
    list_any, count_ref, x_any, bias_any, enc_ref, dec_ref, keep_ref, send_ref, ids_ref,
    list_ref, x_ref, bias_ref, enc_held, dec_held, codes, total, in_sem, enc_sem, dec_sem,
):
    blocks = enc_ref.shape[1] // BLOCK
    list_load = pltpu.make_async_copy(list_any, list_ref, in_sem.at[0])
    list_load.start()
    loads = [pltpu.make_async_copy(x_any, x_ref, in_sem.at[1]), pltpu.make_async_copy(bias_any, bias_ref, in_sem.at[2])]
    for load in loads:
        load.start()
    where = lax.axis_index("latent")
    first = where * blocks
    total[...] = jnp.zeros_like(total)

    def place_of(n):
        return lax.div(n, 4), pl.ds(pl.multiple_of(lax.rem(n, 4) * BLOCK, BLOCK), BLOCK)

    def rows_of(n):
        return pl.ds(pl.multiple_of(ids_ref[0, n] * BLOCK, BLOCK), BLOCK)

    def enc_copy(n):
        quad, place = place_of(n)
        return pltpu.make_async_copy(enc_ref.at[:, rows_of(n)], enc_held.at[quad, :, place], enc_sem.at[n])

    def dec_copy(n):
        quad, place = place_of(n)
        return pltpu.make_async_copy(dec_ref.at[rows_of(n), :], dec_held.at[quad, place, :], dec_sem.at[n])

    list_load.wait()
    count = count_ref[0, 0]

    def look(slot, n):
        block = list_ref[0, 0, slot] - first
        live = (slot < count) & (block >= 0) & (block < blocks)

        @pl.when(live)
        def _():
            ids_ref[0, n] = block
            enc_copy(n).start()

        return n + live.astype(jnp.int32)

    live_count = lax.fori_loop(0, jnp.minimum(count, list_ref.shape[2]), look, jnp.int32(0))
    ids_ref[0, blocks] = live_count
    lax.fori_loop(0, live_count, lambda n, c: (dec_copy(n).start(), c)[1], 0)
    quads = lax.div(live_count + 1, 4)
    last_pair = (lax.rem(live_count, 4) == 1) | (lax.rem(live_count, 4) == 2)

    def clear(n, carry):
        quad, place = place_of(n)
        dec_held[quad, place, :] = jnp.zeros((BLOCK, dec_held.shape[2]), BF16)
        ids_ref[0, n] = ids_ref[0, 0]
        return carry

    lax.fori_loop(live_count, jnp.where(last_pair, 4 * quads + 2, 4 * quads), clear, 0)
    for load in loads:
        load.wait()

    def arrive(copy, quad, size):
        for i in range(size):
            n = 4 * quad + i
            pl.when(n < live_count)(lambda n=n: copy(n).wait())

    def encode(quad, size):
        arrive(enc_copy, quad, size)
        lanes = pl.ds(0, size * BLOCK)
        bias = jnp.concatenate([bias_ref[:, rows_of(4 * quad + i)] for i in range(size)], axis=1)
        pre_act = jnp.dot(x_ref[...], enc_held[quad, :, lanes], preferred_element_type=F32) + bias
        lane = lax.broadcasted_iota(jnp.int32, pre_act.shape, 1)
        used = lane < (live_count - 4 * quad) * BLOCK
        codes[quad, :, lanes] = jnp.where(used, jnp.maximum(pre_act, 0.0), 0.0).astype(BF16)

    def decode(pair, carry):
        quad, lanes = lax.div(pair, 2), pl.ds(pl.multiple_of(lax.rem(pair, 2) * PAIR, PAIR), PAIR)
        for n in (2 * pair, 2 * pair + 1):
            pl.when(n < live_count)(lambda n=n: dec_copy(n).wait())
        total[...] += jnp.dot(codes[quad, :, lanes], dec_held[quad, lanes, :], preferred_element_type=F32)
        return carry

    lax.fori_loop(0, quads, lambda quad, c: (encode(quad, 4), c)[1], 0)
    pl.when(last_pair)(lambda: encode(quads, 2))
    lax.fori_loop(0, lax.div(live_count + 1, 2), decode, 0)

    rows = keep_ref.shape[0]
    core = lax.rem(where, 2)
    keep_ref[...] = total[pl.ds(pl.multiple_of(core * rows, rows), rows), :]
    send_ref[...] = total[pl.ds(pl.multiple_of((1 - core) * rows, rows), rows), :].astype(BF16)


def finish(
    got_ref, before_ref, after_ref, all_ref, there_square_ref, after_square_ref, gain_ref, target_ref,
    message_ref, stay_ref, send_ref,
):
    got = got_ref[...].astype(F32)
    width = got.shape[1]
    low = (lax.axis_index("layer") & (lax.axis_size("layer") // 2)) == 0
    fitted = gain_ref[...] * jnp.where(low, before_ref[...], before_ref[...] + got)
    error_term = fitted - target_ref[...].astype(F32)
    squares = error_term * error_term
    added = functools.reduce(add_terms, [squares[:, i : i + BLOCK] for i in range(0, width - BLOCK + 1, BLOCK)])
    rest = width % BLOCK
    if rest:
        zeros = jnp.zeros((squares.shape[0], BLOCK - rest), F32)
        added = added + jnp.concatenate([squares[:, width - rest :], zeros], axis=1)
    entering = jnp.where(low, there_square_ref[...] * all_ref[...] + got, after_square_ref[...] * got)
    message_ref[:, :width] = (after_ref[...] + entering).astype(BF16)
    message_ref[:, width:] = added.astype(BF16)
    left, right = fitted[:, : width // 2].astype(BF16), fitted[:, width // 2 :].astype(BF16)
    first = (lax.axis_index("latent") & 1) == 0
    stay_ref[...] = jnp.where(first, left, right)
    send_ref[...] = jnp.where(first, right, left)


def add_terms(one, two):
    return one + two


def rows_of(dec_ref, block, half):
    cut = dec_ref.shape[1] // 2
    return dec_ref.at[pl.ds(pl.multiple_of(block * BLOCK, BLOCK), BLOCK), pl.ds(pl.multiple_of(half * cut, cut), cut)]


def place_of(n):
    return lax.div(n, 2), pl.ds(pl.multiple_of(lax.rem(n, 2) * BLOCK, BLOCK), BLOCK)


def by_core(core, mine, theirs, held):
    rows = mine.shape[0]
    held[pl.ds(pl.multiple_of(core * rows, rows), rows), :] = mine
    held[pl.ds(pl.multiple_of((1 - core) * rows, rows), rows), :] = theirs


def times_rows(grad, rows):
    return lax.dot_general(grad, rows, (((1,), (1,)), ((), ())), preferred_element_type=F32)


def near_gradient(top, ids_ref, own_ref, near_ref, dec_ref, part_ref, far_kept, grad, dec_near, near_sem, far_sem):
    blocks = near_sem.shape[0]
    kept, _, cut = far_kept.shape
    latent = lax.axis_index("latent")
    here = lax.div(latent & top, top)
    live_count = ids_ref[0, blocks]
    far_count = jnp.minimum(live_count, 2 * kept)

    def near_copy(n):
        pair, place = place_of(n)
        return pltpu.make_async_copy(rows_of(dec_ref, ids_ref[0, n], here), dec_near.at[pair, place, :], near_sem.at[n])

    def far_copy(n):
        pair, place = place_of(n)
        return pltpu.make_async_copy(rows_of(dec_ref, ids_ref[0, n], 1 - here), far_kept.at[pair, place, :], far_sem.at[n])

    lax.fori_loop(0, live_count, lambda n, c: (near_copy(n).start(), c)[1], 0)
    lax.fori_loop(0, far_count, lambda n, c: (far_copy(n).start(), c)[1], 0)
    by_core(latent & 1, own_ref[:, :cut], near_ref[:, :cut], grad)

    def step(pair, carry):
        n = 2 * pair
        near_copy(n).wait()
        pl.when(n + 1 < live_count)(lambda: near_copy(n + 1).wait())
        part_ref[pair] = times_rows(grad[...], dec_near[pair])
        return carry

    lax.fori_loop(0, lax.div(live_count + 1, 2), step, 0)
    lax.fori_loop(0, far_count, lambda n, c: (far_copy(n).wait(), c)[1], 0)


def code_gradient(
    top, ids_ref, own_ref, got_ref, far_ref, stay_ref, other_ref, part_ref, far_kept, dec_ref,
    out_ref, recon_ref, mean_ref, grad, fitted, dec_far, far_sem,
):
    blocks = far_sem.shape[0]
    kept, _, cut = far_kept.shape
    latent = lax.axis_index("latent")
    there = 1 - lax.div(latent & top, top)
    core = latent & 1
    live_count = ids_ref[0, blocks]
    pairs = lax.div(live_count + 1, 2)

    def far_copy(n):
        pair, place = place_of(n - 2 * kept)
        return pltpu.make_async_copy(rows_of(dec_ref, ids_ref[0, n], there), dec_far.at[pair, place, :], far_sem.at[n])

    lax.fori_loop(2 * kept, live_count, lambda n, c: (far_copy(n).start(), c)[1], 0)
    by_core(core, got_ref[:, :cut], far_ref[:, :cut], grad)
    out_ref[...] = jnp.zeros_like(out_ref)

    def store(pair, product):
        n = 2 * pair
        out_ref[:, pl.ds(pl.multiple_of(ids_ref[0, n] * BLOCK, BLOCK), BLOCK)] = product[:, :BLOCK]

        @pl.when(n + 1 < live_count)
        def _():
            out_ref[:, pl.ds(pl.multiple_of(ids_ref[0, n + 1] * BLOCK, BLOCK), BLOCK)] = product[:, BLOCK:]

    def step(pair, carry):
        store(pair, (part_ref[pair] + times_rows(grad[...], far_kept[pair])).astype(BF16))
        return carry

    def fetched(pair, carry):
        n = 2 * pair
        far_copy(n).wait()
        pl.when(n + 1 < live_count)(lambda: far_copy(n + 1).wait())
        store(pair, (part_ref[pair] + times_rows(grad[...], dec_far[pair - kept])).astype(BF16))
        return carry

    lax.fori_loop(0, jnp.minimum(pairs, kept), step, 0)
    lax.fori_loop(kept, pairs, fetched, 0)
    columns = stay_ref.shape[1]
    by_core(core, stay_ref[...].astype(F32), other_ref[:, :columns].astype(F32), fitted)
    recon_ref[...] = jnp.transpose(fitted[...]).astype(BF16)
    squares = sum(ref[:, cut:].astype(F32) for ref in (own_ref, got_ref, far_ref)) + other_ref[:, columns:].astype(F32)
    total = jnp.sum(jnp.sum(squares, axis=0, keepdims=True), axis=1, keepdims=True)
    mean_ref[...] = total / (grad.shape[0] * 2 * cut)


def swap(value, axis, bit):
    size = lax.axis_size(axis)
    return lax.ppermute(value, axis, [(i, i ^ bit) for i in range(size)])


def in_hbm(value):
    return pltpu.with_memory_space_constraint(value, pltpu.HBM)


def part(value, start, size, axis):
    return lax.dynamic_slice_in_dim(value, start, size, axis)


def encode_call(block_list, block_count, x, bias, enc, dec):
    tok_rows, model_width = x.shape
    local_latents = enc.shape[1]
    blocks = local_latents // BLOCK
    quad_slots = (blocks + 3) // 4
    rows = tok_rows // 2
    vmem = pl.BlockSpec(memory_space=pltpu.VMEM)
    smem = pl.BlockSpec(memory_space=pltpu.SMEM)
    anyw = pl.BlockSpec(memory_space=pl.ANY)
    return pl.pallas_call(
        encode_decode,
        out_shape=(
            pltpu.VMEM((rows, model_width), F32),
            pltpu.VMEM((rows, model_width), BF16),
            pltpu.SMEM((1, blocks + 1), jnp.int32),
        ),
        in_specs=[anyw, smem, anyw, anyw, anyw, anyw],
        out_specs=(vmem, vmem, smem),
        scratch_shapes=[
            pltpu.SMEM(block_list.shape, jnp.int32),
            pltpu.VMEM((tok_rows, model_width), BF16),
            pltpu.VMEM((1, local_latents), F32),
            pltpu.VMEM((quad_slots, model_width, 4 * BLOCK), BF16),
            pltpu.VMEM((quad_slots, 4 * BLOCK, model_width), BF16),
            pltpu.VMEM((quad_slots, tok_rows, 4 * BLOCK), BF16),
            pltpu.VMEM((tok_rows, model_width), F32),
            pltpu.SemaphoreType.DMA((3,)),
            pltpu.SemaphoreType.DMA((blocks,)),
            pltpu.SemaphoreType.DMA((blocks,)),
        ],
        compiler_params=pltpu.CompilerParams(vmem_limit_bytes=32 << 20),
        name="encode_decode",
    )(block_list, block_count, x, bias, enc, dec)


def local(residuals, targets, enc_weight, enc_bias, dec_weight, out_gain, block_list, block_count):
    tok_rows, model_width = residuals.shape[1:]
    local_latents = enc_weight.shape[2]
    blocks = local_latents // BLOCK
    pair_slots = (blocks + 1) // 2
    kept = min(KEPT_PAIRS, pair_slots)
    more = max(pair_slots - kept, 1)
    layers, latents = lax.axis_size("layer"), lax.axis_size("latent")
    layer, latent = lax.axis_index("layer"), lax.axis_index("latent")
    core = latent % 2
    rows = tok_rows // 2
    chips = latents // 2
    width = model_width // chips
    column = (latent // 2) * width

    gain = part(out_gain, column, width, 1)
    target = part(part(targets[0], core * rows, rows, 0), column, width, 1)
    terms, left = [], gain
    for _ in range(3):
        terms.append(lax.reduce_precision(left, 8, 7))
        left = left - terms[-1]
    beside = jnp.concatenate([target, *[term.astype(BF16) for term in terms], jnp.zeros((13, width), BF16)], axis=0)
    layer_bits = [1 << s for s in range((layers - 1).bit_length())]
    chip_bits = [1 << s for s in range((chips - 1).bit_length(), 0, -1)]

    dec_hbm = in_hbm(dec_weight[0])
    vmem = pl.BlockSpec(memory_space=pltpu.VMEM)
    smem = pl.BlockSpec(memory_space=pltpu.SMEM)
    anyw = pl.BlockSpec(memory_space=pl.ANY)
    keep, send, ids = encode_call(
        in_hbm(block_list), block_count, in_hbm(residuals[0]), in_hbm(enc_bias), in_hbm(enc_weight[0]), dec_hbm
    )

    held = keep + swap(send, "latent", 1).astype(F32)
    for bit in chip_bits:
        half = held.shape[1] // 2
        upper = (latent & bit) != 0
        away = jnp.where(upper, held[:, :half], held[:, half:]).astype(BF16)
        mine = jnp.where(upper, held[:, half:], held[:, :half])
        if bit == chip_bits[-1]:
            beside = swap(beside, "layer", 1)
        held = mine + swap(away, "latent", bit).astype(F32)
    own = held
    near = swap(own.astype(BF16), "layer", 1).astype(F32)
    near_target = beside[:rows]
    near_gain = sum(beside[rows + i : rows + i + 1].astype(F32) for i in range(3))
    square = gain * gain
    near_square = near_gain * near_gain
    all_square = square + near_square

    low = (layer & 1) == 0
    own_error = square * own - gain * target.astype(F32)
    near_error = near_square * near - near_gain * near_target.astype(F32)
    before = jnp.where(low, own, own + near)
    after = jnp.where(low, own_error + near_square * own + near_error, own_error + square * near)
    after_square = jnp.where(low, square + near_square, square)
    all_before = own + near
    all_after = own_error + near_error + jnp.where(low, near_square * own, square * near)
    for step in layer_bits[1:]:
        low = (layer & step) == 0
        there_square = swap(all_square, "layer", step)
        if step == layer_bits[-1]:
            got = swap(jnp.where(low, all_before, all_after).astype(BF16), "layer", step)
            break
        there_before = swap(all_before.astype(BF16), "layer", step).astype(F32)
        there_after = swap(all_after.astype(BF16), "layer", step).astype(F32)
        before, after = (
            jnp.where(low, before, before + there_before),
            jnp.where(low, after + there_square * all_before + there_after, after + after_square * there_before),
        )
        after_square = jnp.where(low, after_square + there_square, after_square)
        all_before, all_after = (
            all_before + there_before,
            all_after + there_after + jnp.where(low, there_square * all_before, all_square * there_before),
        )
        all_square = all_square + there_square

    columns = width // 2
    message, stay, send = pl.pallas_call(
        finish,
        out_shape=(
            pltpu.VMEM((rows, width + BLOCK), BF16),
            pltpu.VMEM((rows, columns), BF16),
            pltpu.VMEM((rows, columns), BF16),
        ),
        in_specs=[vmem] * 8,
        out_specs=(vmem, vmem, vmem),
        compiler_params=pltpu.CompilerParams(vmem_limit_bytes=16 << 20),
        name="finish",
    )(got, before, after, all_before, there_square, after_square, gain, target)

    for bit in reversed(chip_bits[1:]):
        upper = (latent & bit) != 0
        got = swap(message, "latent", bit)
        cut = message.shape[1] - BLOCK
        here, there = message[:, :cut], got[:, :cut]
        squares = (message[:, cut:].astype(F32) + got[:, cut:].astype(F32)).astype(BF16)
        message = jnp.concatenate([jnp.where(upper, there, here), jnp.where(upper, here, there), squares], axis=1)
    top, cut = chip_bits[0], model_width // 2
    got = swap(message, "latent", top)
    near = swap(message[:, :cut], "latent", 1)
    send = jnp.concatenate([send, message[:, cut:]], axis=1)
    near_part, far_kept = pl.pallas_call(
        functools.partial(near_gradient, top),
        out_shape=(pltpu.VMEM((pair_slots, tok_rows, PAIR), F32), pltpu.VMEM((kept, PAIR, cut), BF16)),
        in_specs=[smem, vmem, vmem, anyw],
        out_specs=(vmem, vmem),
        scratch_shapes=[
            pltpu.VMEM((tok_rows, cut), BF16),
            pltpu.VMEM((pair_slots, PAIR, cut), BF16),
            pltpu.SemaphoreType.DMA((blocks,)),
            pltpu.SemaphoreType.DMA((blocks,)),
        ],
        compiler_params=pltpu.CompilerParams(vmem_limit_bytes=24 << 20),
        name="near_gradient",
    )(ids, message, near, dec_hbm)
    got, near_part, send = lax.optimization_barrier((got, near_part, send))
    far = swap(got, "latent", 1)
    other = swap(send, "latent", 1)

    code_grad, recon, loss = pl.pallas_call(
        functools.partial(code_gradient, top),
        out_shape=(
            jax.ShapeDtypeStruct((tok_rows, local_latents), BF16),
            jax.ShapeDtypeStruct((columns, tok_rows), BF16),
            jax.ShapeDtypeStruct((1, 1), F32),
        ),
        in_specs=[smem] + [vmem] * 7 + [anyw],
        out_specs=(vmem, vmem, vmem),
        scratch_shapes=[
            pltpu.VMEM((tok_rows, cut), BF16),
            pltpu.VMEM((tok_rows, columns), F32),
            pltpu.VMEM((more, PAIR, cut), BF16),
            pltpu.SemaphoreType.DMA((blocks,)),
        ],
        compiler_params=pltpu.CompilerParams(vmem_limit_bytes=16 << 20),
        name="code_gradient",
    )(ids, message, got, far, stay, other, *[pltpu.with_memory_space_constraint(a, pltpu.VMEM) for a in (near_part, far_kept)], dec_hbm)
    return recon.T[None], code_grad[None], loss


def solution(mesh):
    placed = (
        P("layer", "groups", None),
        P("layer", "groups", None),
        P("layer", None, "latent"),
        P("layer", "latent"),
        P("layer", "latent", None),
        P("layer", None),
        P("layer", "groups", None),
        P("layer", "groups"),
    )
    return jax.shard_map(
        local,
        mesh=mesh,
        in_specs=placed,
        out_specs=(
            P("layer", "groups", "latent"),
            P("layer", "groups", "latent"),
            P("groups", "layer"),
        ),
        check_vma=False,
    )
```

```python
import functools

import jax
import jax.numpy as jnp
from jax import lax
from jax.experimental import pallas as pl
from jax.experimental.pallas import tpu as pltpu
from jax.sharding import PartitionSpec as P

BLOCK = 128
PAIR = 2 * BLOCK
KEPT = 2
F32 = jnp.float32
BF16 = jnp.bfloat16


def encode_decode(
    list_any, count_ref, x_any, bias_any, target_any, gain_any, enc_ref, dec_ref,
    keep_ref, send_ref, ids_ref, beside_ref, own_gain_ref,
    list_ref, x_ref, bias_ref, target_ref, gain_ref, enc_held, dec_held, codes, total, in_sem, enc_sem, dec_sem,
):
    blocks = enc_ref.shape[1] // BLOCK
    list_load = pltpu.make_async_copy(list_any, list_ref, in_sem.at[0])
    list_load.start()
    where = lax.axis_index("latent")
    first = where * blocks
    core = lax.rem(where, 2)
    rows = keep_ref.shape[0]
    mine = pl.ds(pl.multiple_of(core * rows, rows), rows)
    loads = [
        pltpu.make_async_copy(x_any, x_ref, in_sem.at[1]),
        pltpu.make_async_copy(bias_any, bias_ref, in_sem.at[2]),
        pltpu.make_async_copy(target_any.at[mine, :], target_ref, in_sem.at[3]),
        pltpu.make_async_copy(gain_any, gain_ref, in_sem.at[4]),
    ]
    for load in loads:
        load.start()
    total[...] = jnp.zeros_like(total)

    def place_of(n):
        return lax.div(n, 4), pl.ds(pl.multiple_of(lax.rem(n, 4) * BLOCK, BLOCK), BLOCK)

    def rows_of(n):
        return pl.ds(pl.multiple_of(ids_ref[0, n] * BLOCK, BLOCK), BLOCK)

    def enc_copy(n):
        quad, place = place_of(n)
        return pltpu.make_async_copy(enc_ref.at[:, rows_of(n)], enc_held.at[quad, :, place], enc_sem.at[n])

    def dec_copy(n):
        quad, place = place_of(n)
        return pltpu.make_async_copy(dec_ref.at[rows_of(n), :], dec_held.at[quad, place, :], dec_sem.at[n])

    list_load.wait()
    count = count_ref[0, 0]

    def look(slot, n):
        block = list_ref[0, 0, slot] - first
        live = (slot < count) & (block >= 0) & (block < blocks)

        @pl.when(live)
        def _():
            ids_ref[0, n] = block
            enc_copy(n).start()

        return n + live.astype(jnp.int32)

    live_count = lax.fori_loop(0, jnp.minimum(count, list_ref.shape[2]), look, jnp.int32(0))
    ids_ref[0, blocks] = live_count
    lax.fori_loop(0, live_count, lambda n, c: (dec_copy(n).start(), c)[1], 0)
    quads = lax.div(live_count + 1, 4)
    last_pair = (lax.rem(live_count, 4) == 1) | (lax.rem(live_count, 4) == 2)

    def clear(n, carry):
        quad, place = place_of(n)
        dec_held[quad, place, :] = jnp.zeros((BLOCK, dec_held.shape[2]), BF16)
        ids_ref[0, n] = ids_ref[0, 0]
        return carry

    lax.fori_loop(live_count, jnp.where(last_pair, 4 * quads + 2, 4 * quads), clear, 0)
    for load in loads:
        load.wait()

    width = own_gain_ref.shape[1]
    for chip in range(target_ref.shape[1] // width):

        @pl.when(lax.div(where, 2) == chip)
        def _(columns=slice(chip * width, (chip + 1) * width)):
            beside_ref[:rows, :] = target_ref[:, columns]
            own_gain_ref[...] = gain_ref[:, columns]

    left, terms = own_gain_ref[...], []
    for _ in range(3):
        terms.append(left.astype(BF16).astype(F32))
        left = left - terms[-1]
    row = lax.broadcasted_iota(jnp.int32, (beside_ref.shape[0] - rows, width), 0)
    beside_ref[rows:, :] = sum(jnp.where(row == i, term, 0.0) for i, term in enumerate(terms)).astype(BF16)

    def encode(n, size):
        for i in range(size):
            pl.when(n + i < live_count)(lambda i=i: enc_copy(n + i).wait())
        quad = lax.div(n, 4)
        lanes = pl.ds(pl.multiple_of(lax.rem(n, 4) * BLOCK, size * BLOCK), size * BLOCK)
        bias = jnp.concatenate([bias_ref[:, rows_of(n + i)] for i in range(size)], axis=1)
        pre_act = jnp.dot(x_ref[...], enc_held[quad, :, lanes], preferred_element_type=F32) + bias
        lane = lax.broadcasted_iota(jnp.int32, pre_act.shape, 1)
        used = lane < (live_count - n) * BLOCK
        codes[quad, :, lanes] = jnp.where(used, jnp.maximum(pre_act, 0.0), 0.0).astype(BF16)

    def decode(pair, carry):
        quad, lanes = lax.div(pair, 2), pl.ds(pl.multiple_of(lax.rem(pair, 2) * PAIR, PAIR), PAIR)
        for n in (2 * pair, 2 * pair + 1):
            pl.when(n < live_count)(lambda n=n: dec_copy(n).wait())
        total[...] += jnp.dot(codes[quad, :, lanes], dec_held[quad, lanes, :], preferred_element_type=F32)
        return carry

    pairs = lax.div(live_count + 1, 2)
    fours = jnp.where(live_count <= 4, 0, quads)
    lax.fori_loop(0, fours, lambda quad, c: (encode(4 * quad, 4), c)[1], 0)
    lax.fori_loop(2 * fours, pairs, lambda pair, c: (encode(2 * pair, 2), c)[1], 0)
    lax.fori_loop(0, pairs, decode, 0)

    keep_ref[...] = total[mine, :]
    send_ref[...] = total[pl.ds(pl.multiple_of((1 - core) * rows, rows), rows), :].astype(BF16)


def finish(
    got_ref, before_ref, after_ref, all_ref, there_square_ref, after_square_ref, gain_ref, target_ref,
    message_ref, stay_ref, send_ref,
):
    got = got_ref[...].astype(F32)
    width = got.shape[1]
    low = (lax.axis_index("layer") & (lax.axis_size("layer") // 2)) == 0
    fitted = gain_ref[...] * jnp.where(low, before_ref[...], before_ref[...] + got)
    error_term = fitted - target_ref[: got.shape[0], :].astype(F32)
    squares = error_term * error_term
    added = functools.reduce(add_terms, [squares[:, i : i + BLOCK] for i in range(0, width - BLOCK + 1, BLOCK)])
    rest = width % BLOCK
    if rest:
        zeros = jnp.zeros((squares.shape[0], BLOCK - rest), F32)
        added = added + jnp.concatenate([squares[:, width - rest :], zeros], axis=1)
    entering = jnp.where(low, there_square_ref[...] * all_ref[...] + got, after_square_ref[...] * got)
    message_ref[:, :width] = (after_ref[...] + entering).astype(BF16)
    message_ref[:, width:] = added.astype(BF16)
    left, right = fitted[:, : width // 2].astype(BF16), fitted[:, width // 2 :].astype(BF16)
    first = (lax.axis_index("latent") & 1) == 0
    stay_ref[...] = jnp.where(first, left, right)
    send_ref[...] = jnp.where(first, right, left)


def add_terms(one, two):
    return one + two


def rows_of(dec_ref, block, half):
    cut = dec_ref.shape[1] // 2
    return dec_ref.at[pl.ds(pl.multiple_of(block * BLOCK, BLOCK), BLOCK), pl.ds(pl.multiple_of(half * cut, cut), cut)]


def in_quads(n):
    return lax.div(n, 4), pl.ds(pl.multiple_of(lax.rem(n, 4) * BLOCK, BLOCK), BLOCK)


def quads_of(live_count):
    rest = lax.rem(live_count, 4)
    return lax.div(live_count + 1, 4), (rest == 1) | (rest == 2)


def by_core(core, mine, theirs, held):
    rows = mine.shape[0]
    held[pl.ds(pl.multiple_of(core * rows, rows), rows), :] = mine
    held[pl.ds(pl.multiple_of((1 - core) * rows, rows), rows), :] = theirs


def times_rows(grad, rows):
    return lax.dot_general(grad, rows, (((1,), (1,)), ((), ())), preferred_element_type=F32)


def near_gradient(top, ids_ref, own_ref, near_ref, dec_ref, part_ref, far_kept, grad, dec_near, near_sem, far_sem):
    blocks = near_sem.shape[0]
    kept, _, cut = far_kept.shape
    latent = lax.axis_index("latent")
    here = lax.div(latent & top, top)
    live_count = ids_ref[0, blocks]
    far_count = jnp.minimum(live_count, 4 * kept)

    def near_copy(n):
        quad, place = in_quads(n)
        return pltpu.make_async_copy(rows_of(dec_ref, ids_ref[0, n], here), dec_near.at[quad, place, :], near_sem.at[n])

    def far_copy(n):
        quad, place = in_quads(n)
        return pltpu.make_async_copy(rows_of(dec_ref, ids_ref[0, n], 1 - here), far_kept.at[quad, place, :], far_sem.at[n])

    lax.fori_loop(0, live_count, lambda n, c: (near_copy(n).start(), c)[1], 0)
    lax.fori_loop(0, far_count, lambda n, c: (far_copy(n).start(), c)[1], 0)
    by_core(latent & 1, own_ref[:, :cut], near_ref[:, :cut], grad)

    def multiply(quad, size):
        for n in [4 * quad + i for i in range(size)]:
            pl.when(n < live_count)(lambda n=n: near_copy(n).wait())
        places = pl.ds(0, size * BLOCK)
        part_ref[quad, :, places] = times_rows(grad[...], dec_near[quad, places, :])

    quads, last_pair = quads_of(live_count)
    lax.fori_loop(0, quads, lambda quad, c: (multiply(quad, 4), c)[1], 0)
    pl.when(last_pair)(lambda: multiply(quads, 2))
    lax.fori_loop(0, far_count, lambda n, c: (far_copy(n).wait(), c)[1], 0)


def code_gradient(
    top, ids_ref, own_ref, got_ref, far_ref, stay_ref, other_ref, part_ref, far_kept, dec_ref,
    out_ref, recon_ref, mean_ref, grad, fitted, dec_far, far_sem,
):
    blocks = far_sem.shape[0]
    kept, _, cut = far_kept.shape
    latent = lax.axis_index("latent")
    there = 1 - lax.div(latent & top, top)
    core = latent & 1
    live_count = ids_ref[0, blocks]

    def far_copy(n):
        quad, place = in_quads(n)
        return pltpu.make_async_copy(rows_of(dec_ref, ids_ref[0, n], there), dec_far.at[quad - kept, place, :], far_sem.at[n])

    lax.fori_loop(4 * kept, live_count, lambda n, c: (far_copy(n).start(), c)[1], 0)
    by_core(core, got_ref[:, :cut], far_ref[:, :cut], grad)
    out_ref[...] = jnp.zeros_like(out_ref)

    def multiply(quad, size, held, offset):
        blocks_here = [4 * quad + i for i in range(size)]
        if offset:
            for n in blocks_here:
                pl.when(n < live_count)(lambda n=n: far_copy(n).wait())
        places = pl.ds(0, size * BLOCK)
        product = (part_ref[quad, :, places] + times_rows(grad[...], held[quad - offset, places, :])).astype(BF16)
        for i, n in enumerate(blocks_here):

            @pl.when(n < live_count)
            def _(i=i, n=n):
                lanes = pl.ds(pl.multiple_of(ids_ref[0, n] * BLOCK, BLOCK), BLOCK)
                out_ref[:, lanes] = product[:, i * BLOCK : (i + 1) * BLOCK]

    quads, last_pair = quads_of(live_count)
    lax.fori_loop(0, jnp.minimum(quads, kept), lambda quad, c: (multiply(quad, 4, far_kept, 0), c)[1], 0)
    lax.fori_loop(kept, quads, lambda quad, c: (multiply(quad, 4, dec_far, kept), c)[1], 0)
    pl.when(last_pair & (quads < kept))(lambda: multiply(quads, 2, far_kept, 0))
    pl.when(last_pair & (quads >= kept))(lambda: multiply(quads, 2, dec_far, kept))
    columns = stay_ref.shape[1]
    by_core(core, stay_ref[...].astype(F32), other_ref[:, :columns].astype(F32), fitted)
    recon_ref[...] = jnp.transpose(fitted[...]).astype(BF16)
    squares = sum(ref[:, cut:].astype(F32) for ref in (own_ref, got_ref, far_ref)) + other_ref[:, columns:].astype(F32)
    total = jnp.sum(jnp.sum(squares, axis=0, keepdims=True), axis=1, keepdims=True)
    mean_ref[...] = total / (grad.shape[0] * 2 * cut)


def swap(value, axis, bit):
    size = lax.axis_size(axis)
    return lax.ppermute(value, axis, [(i, i ^ bit) for i in range(size)])


def in_hbm(value):
    return pltpu.with_memory_space_constraint(value, pltpu.HBM)


def part(value, start, size, axis):
    return lax.dynamic_slice_in_dim(value, start, size, axis)


def encode_call(block_list, block_count, x, bias, targets, gain, enc, dec, width):
    tok_rows, model_width = x.shape
    local_latents = enc.shape[1]
    blocks = local_latents // BLOCK
    quad_slots = (blocks + 3) // 4
    rows = tok_rows // 2
    vmem = pl.BlockSpec(memory_space=pltpu.VMEM)
    smem = pl.BlockSpec(memory_space=pltpu.SMEM)
    anyw = pl.BlockSpec(memory_space=pl.ANY)
    return pl.pallas_call(
        encode_decode,
        out_shape=(
            pltpu.VMEM((rows, model_width), F32),
            pltpu.VMEM((rows, model_width), BF16),
            pltpu.SMEM((1, blocks + 1), jnp.int32),
            pltpu.VMEM((rows + 16, width), BF16),
            pltpu.VMEM((1, width), F32),
        ),
        in_specs=[anyw, smem] + [anyw] * 6,
        out_specs=(vmem, vmem, smem, vmem, vmem),
        scratch_shapes=[
            pltpu.SMEM(block_list.shape, jnp.int32),
            pltpu.VMEM((tok_rows, model_width), BF16),
            pltpu.VMEM((1, local_latents), F32),
            pltpu.VMEM((rows, model_width), BF16),
            pltpu.VMEM((1, model_width), F32),
            pltpu.VMEM((quad_slots, model_width, 4 * BLOCK), BF16),
            pltpu.VMEM((quad_slots, 4 * BLOCK, model_width), BF16),
            pltpu.VMEM((quad_slots, tok_rows, 4 * BLOCK), BF16),
            pltpu.VMEM((tok_rows, model_width), F32),
            pltpu.SemaphoreType.DMA((5,)),
            pltpu.SemaphoreType.DMA((blocks,)),
            pltpu.SemaphoreType.DMA((blocks,)),
        ],
        compiler_params=pltpu.CompilerParams(vmem_limit_bytes=32 << 20),
        name="encode_decode",
    )(block_list, block_count, x, bias, targets, gain, enc, dec)


def local(residuals, targets, enc_weight, enc_bias, dec_weight, out_gain, block_list, block_count):
    tok_rows, model_width = residuals.shape[1:]
    local_latents = enc_weight.shape[2]
    blocks = local_latents // BLOCK
    slots = (blocks + 3) // 4
    kept = min(KEPT, slots)
    more = max(slots - kept, 1)
    quad = 4 * BLOCK
    layers, latents = lax.axis_size("layer"), lax.axis_size("latent")
    layer, latent = lax.axis_index("layer"), lax.axis_index("latent")
    core = latent % 2
    rows = tok_rows // 2
    chips = latents // 2
    width = model_width // chips
    column = (latent // 2) * width

    layer_bits = [1 << s for s in range((layers - 1).bit_length())]
    chip_bits = [1 << s for s in range((chips - 1).bit_length(), 0, -1)]

    dec_hbm = in_hbm(dec_weight[0])
    vmem = pl.BlockSpec(memory_space=pltpu.VMEM)
    smem = pl.BlockSpec(memory_space=pltpu.SMEM)
    anyw = pl.BlockSpec(memory_space=pl.ANY)
    keep, send, ids, beside, gain = encode_call(
        in_hbm(block_list), block_count, in_hbm(residuals[0]), in_hbm(enc_bias), in_hbm(targets[0]), in_hbm(out_gain),
        in_hbm(enc_weight[0]), dec_hbm, width,
    )

    held = keep + swap(send, "latent", 1).astype(F32)
    for bit in chip_bits:
        half = held.shape[1] // 2
        upper = (latent & bit) != 0
        away = jnp.where(upper, held[:, :half], held[:, half:]).astype(BF16)
        mine = jnp.where(upper, held[:, half:], held[:, :half])
        if bit == chip_bits[-1]:
            near_beside = swap(beside, "layer", 1)
        held = mine + swap(away, "latent", bit).astype(F32)
    own = held
    near = swap(own.astype(BF16), "layer", 1).astype(F32)
    target = beside[:rows]
    near_target = near_beside[:rows]
    near_gain = sum(near_beside[rows + i : rows + i + 1].astype(F32) for i in range(3))
    square = gain * gain
    near_square = near_gain * near_gain
    all_square = square + near_square

    low = (layer & 1) == 0
    own_error = square * own - gain * target.astype(F32)
    near_error = near_square * near - near_gain * near_target.astype(F32)
    before = jnp.where(low, own, own + near)
    after = jnp.where(low, own_error + near_square * own + near_error, own_error + square * near)
    after_square = jnp.where(low, square + near_square, square)
    all_before = own + near
    all_after = own_error + near_error + jnp.where(low, near_square * own, square * near)
    for step in layer_bits[1:]:
        low = (layer & step) == 0
        there_square = swap(all_square, "layer", step)
        if step == layer_bits[-1]:
            got = swap(jnp.where(low, all_before, all_after).astype(BF16), "layer", step)
            break
        there_before = swap(all_before.astype(BF16), "layer", step).astype(F32)
        there_after = swap(all_after.astype(BF16), "layer", step).astype(F32)
        before, after = (
            jnp.where(low, before, before + there_before),
            jnp.where(low, after + there_square * all_before + there_after, after + after_square * there_before),
        )
        after_square = jnp.where(low, after_square + there_square, after_square)
        all_before, all_after = (
            all_before + there_before,
            all_after + there_after + jnp.where(low, there_square * all_before, all_square * there_before),
        )
        all_square = all_square + there_square

    columns = width // 2
    message, stay, send = pl.pallas_call(
        finish,
        out_shape=(
            pltpu.VMEM((rows, width + BLOCK), BF16),
            pltpu.VMEM((rows, columns), BF16),
            pltpu.VMEM((rows, columns), BF16),
        ),
        in_specs=[vmem] * 8,
        out_specs=(vmem, vmem, vmem),
        compiler_params=pltpu.CompilerParams(vmem_limit_bytes=16 << 20),
        name="finish",
    )(got, before, after, all_before, there_square, after_square, gain, beside)

    for bit in reversed(chip_bits[1:]):
        upper = (latent & bit) != 0
        got = swap(message, "latent", bit)
        cut = message.shape[1] - BLOCK
        here, there = message[:, :cut], got[:, :cut]
        squares = (message[:, cut:].astype(F32) + got[:, cut:].astype(F32)).astype(BF16)
        message = jnp.concatenate([jnp.where(upper, there, here), jnp.where(upper, here, there), squares], axis=1)
    top, cut = chip_bits[0], model_width // 2
    got = swap(message, "latent", top)
    near = swap(message[:, :cut], "latent", 1)
    send = jnp.concatenate([send, message[:, cut:]], axis=1)
    near_part, far_kept = pl.pallas_call(
        functools.partial(near_gradient, top),
        out_shape=(pltpu.VMEM((slots, tok_rows, quad), F32), pltpu.VMEM((kept, quad, cut), BF16)),
        in_specs=[smem, vmem, vmem, anyw],
        out_specs=(vmem, vmem),
        scratch_shapes=[
            pltpu.VMEM((tok_rows, cut), BF16),
            pltpu.VMEM((slots, quad, cut), BF16),
            pltpu.SemaphoreType.DMA((blocks,)),
            pltpu.SemaphoreType.DMA((blocks,)),
        ],
        compiler_params=pltpu.CompilerParams(vmem_limit_bytes=24 << 20),
        name="near_gradient",
    )(ids, message, near, dec_hbm)
    got, near_part, send = lax.optimization_barrier((got, near_part, send))
    far = swap(got, "latent", 1)
    other = swap(send, "latent", 1)

    code_grad, recon, loss = pl.pallas_call(
        functools.partial(code_gradient, top),
        out_shape=(
            jax.ShapeDtypeStruct((tok_rows, local_latents), BF16),
            jax.ShapeDtypeStruct((columns, tok_rows), BF16),
            jax.ShapeDtypeStruct((1, 1), F32),
        ),
        in_specs=[smem] + [vmem] * 7 + [anyw],
        out_specs=(vmem, vmem, vmem),
        scratch_shapes=[
            pltpu.VMEM((tok_rows, cut), BF16),
            pltpu.VMEM((tok_rows, columns), F32),
            pltpu.VMEM((more, quad, cut), BF16),
            pltpu.SemaphoreType.DMA((blocks,)),
        ],
        compiler_params=pltpu.CompilerParams(vmem_limit_bytes=16 << 20),
        name="code_gradient",
    )(ids, message, got, far, stay, other, *[pltpu.with_memory_space_constraint(a, pltpu.VMEM) for a in (near_part, far_kept)], dec_hbm)
    return recon.T[None], code_grad[None], loss


def solution(mesh):
    placed = (
        P("layer", "groups", None),
        P("layer", "groups", None),
        P("layer", None, "latent"),
        P("layer", "latent"),
        P("layer", "latent", None),
        P("layer", None),
        P("layer", "groups", None),
        P("layer", "groups"),
    )
    return jax.shard_map(
        local,
        mesh=mesh,
        in_specs=placed,
        out_specs=(
            P("layer", "groups", "latent"),
            P("layer", "groups", "latent"),
            P("groups", "layer"),
        ),
        check_vma=False,
    )
```

```python
import functools

import jax
import jax.numpy as jnp
from jax import lax
from jax.experimental import pallas as pl
from jax.experimental.pallas import tpu as pltpu
from jax.sharding import PartitionSpec as P

BLOCK = 128
PAIR = 2 * BLOCK
KEPT = 2
F32 = jnp.float32
BF16 = jnp.bfloat16


def encode_decode(
    list_any, count_ref, x_any, bias_any, target_any, gain_any, enc_ref, dec_ref,
    keep_ref, send_ref, ids_ref, beside_ref, own_gain_ref,
    list_ref, x_ref, bias_ref, target_ref, gain_ref, enc_held, dec_held, codes, total, in_sem, enc_sem, dec_sem,
):
    blocks = enc_ref.shape[1] // BLOCK
    list_load = pltpu.make_async_copy(list_any, list_ref, in_sem.at[0])
    list_load.start()
    where = lax.axis_index("latent")
    first = where * blocks
    core = lax.rem(where, 2)
    rows = keep_ref.shape[0]
    mine = pl.ds(pl.multiple_of(core * rows, rows), rows)
    loads = [
        pltpu.make_async_copy(x_any, x_ref, in_sem.at[1]),
        pltpu.make_async_copy(bias_any, bias_ref, in_sem.at[2]),
        pltpu.make_async_copy(target_any.at[mine, :], target_ref, in_sem.at[3]),
        pltpu.make_async_copy(gain_any, gain_ref, in_sem.at[4]),
    ]
    for load in loads:
        load.start()
    total[...] = jnp.zeros_like(total)

    def place_of(n):
        return lax.div(n, 4), pl.ds(pl.multiple_of(lax.rem(n, 4) * BLOCK, BLOCK), BLOCK)

    def rows_of(n):
        return pl.ds(pl.multiple_of(ids_ref[0, n] * BLOCK, BLOCK), BLOCK)

    def enc_copy(n):
        quad, place = place_of(n)
        return pltpu.make_async_copy(enc_ref.at[:, rows_of(n)], enc_held.at[quad, :, place], enc_sem.at[n])

    def dec_copy(n):
        quad, place = place_of(n)
        return pltpu.make_async_copy(dec_ref.at[rows_of(n), :], dec_held.at[quad, place, :], dec_sem.at[n])

    list_load.wait()
    count = count_ref[0, 0]

    def look(slot, n):
        block = list_ref[0, 0, slot] - first
        live = (slot < count) & (block >= 0) & (block < blocks)

        @pl.when(live)
        def _():
            ids_ref[0, n] = block
            enc_copy(n).start()

        return n + live.astype(jnp.int32)

    live_count = lax.fori_loop(0, jnp.minimum(count, list_ref.shape[2]), look, jnp.int32(0))
    ids_ref[0, blocks] = live_count
    lax.fori_loop(0, live_count, lambda n, c: (dec_copy(n).start(), c)[1], 0)
    quads = lax.div(live_count + 1, 4)
    last_pair = (lax.rem(live_count, 4) == 1) | (lax.rem(live_count, 4) == 2)

    def clear(n, carry):
        quad, place = place_of(n)
        dec_held[quad, place, :] = jnp.zeros((BLOCK, dec_held.shape[2]), BF16)
        ids_ref[0, n] = ids_ref[0, 0]
        return carry

    lax.fori_loop(live_count, jnp.where(last_pair, 4 * quads + 2, 4 * quads), clear, 0)
    for load in loads:
        load.wait()

    width = own_gain_ref.shape[1]
    for chip in range(target_ref.shape[1] // width):

        @pl.when(lax.div(where, 2) == chip)
        def _(columns=slice(chip * width, (chip + 1) * width)):
            beside_ref[:rows, :] = target_ref[:, columns]
            own_gain_ref[...] = gain_ref[:, columns]

    left, terms = own_gain_ref[...], []
    for _ in range(3):
        terms.append(left.astype(BF16).astype(F32))
        left = left - terms[-1]
    row = lax.broadcasted_iota(jnp.int32, (beside_ref.shape[0] - rows, width), 0)
    beside_ref[rows:, :] = sum(jnp.where(row == i, term, 0.0) for i, term in enumerate(terms)).astype(BF16)

    def encode(n, size):
        for i in range(size):
            pl.when(n + i < live_count)(lambda i=i: enc_copy(n + i).wait())
        quad = lax.div(n, 4)
        lanes = pl.ds(pl.multiple_of(lax.rem(n, 4) * BLOCK, size * BLOCK), size * BLOCK)
        bias = jnp.concatenate([bias_ref[:, rows_of(n + i)] for i in range(size)], axis=1)
        pre_act = jnp.dot(x_ref[...], enc_held[quad, :, lanes], preferred_element_type=F32) + bias
        lane = lax.broadcasted_iota(jnp.int32, pre_act.shape, 1)
        used = lane < (live_count - n) * BLOCK
        codes[quad, :, lanes] = jnp.where(used, jnp.maximum(pre_act, 0.0), 0.0).astype(BF16)

    def decode(pair, carry):
        quad, lanes = lax.div(pair, 2), pl.ds(pl.multiple_of(lax.rem(pair, 2) * PAIR, PAIR), PAIR)
        for n in (2 * pair, 2 * pair + 1):
            pl.when(n < live_count)(lambda n=n: dec_copy(n).wait())
        total[...] += jnp.dot(codes[quad, :, lanes], dec_held[quad, lanes, :], preferred_element_type=F32)
        return carry

    pairs = lax.div(live_count + 1, 2)
    fours = jnp.where(live_count <= 4, 0, quads)
    lax.fori_loop(0, fours, lambda quad, c: (encode(4 * quad, 4), c)[1], 0)
    lax.fori_loop(2 * fours, pairs, lambda pair, c: (encode(2 * pair, 2), c)[1], 0)
    lax.fori_loop(0, pairs, decode, 0)

    keep_ref[...] = total[mine, :]
    send_ref[...] = total[pl.ds(pl.multiple_of((1 - core) * rows, rows), rows), :].astype(BF16)


def finish(
    got_ref, before_ref, after_ref, all_ref, there_square_ref, after_square_ref, gain_ref, target_ref,
    message_ref, stay_ref, send_ref,
):
    got = got_ref[...].astype(F32)
    width = got.shape[1]
    low = (lax.axis_index("layer") & (lax.axis_size("layer") // 2)) == 0
    fitted = gain_ref[...] * jnp.where(low, before_ref[...], before_ref[...] + got)
    error_term = fitted - target_ref[: got.shape[0], :].astype(F32)
    squares = error_term * error_term
    added = functools.reduce(add_terms, [squares[:, i : i + BLOCK] for i in range(0, width - BLOCK + 1, BLOCK)])
    rest = width % BLOCK
    if rest:
        zeros = jnp.zeros((squares.shape[0], BLOCK - rest), F32)
        added = added + jnp.concatenate([squares[:, width - rest :], zeros], axis=1)
    entering = jnp.where(low, there_square_ref[...] * all_ref[...] + got, after_square_ref[...] * got)
    message_ref[:, :width] = (after_ref[...] + entering).astype(BF16)
    message_ref[:, width:] = added.astype(BF16)
    left, right = fitted[:, : width // 2].astype(BF16), fitted[:, width // 2 :].astype(BF16)
    first = (lax.axis_index("latent") & 1) == 0
    stay_ref[...] = jnp.where(first, left, right)
    send_ref[...] = jnp.where(first, right, left)


def add_terms(one, two):
    return one + two


def rows_of(dec_ref, block, half):
    cut = dec_ref.shape[1] // 2
    return dec_ref.at[pl.ds(pl.multiple_of(block * BLOCK, BLOCK), BLOCK), pl.ds(pl.multiple_of(half * cut, cut), cut)]


def in_quads(n):
    return lax.div(n, 4), pl.ds(pl.multiple_of(lax.rem(n, 4) * BLOCK, BLOCK), BLOCK)


def quads_of(live_count):
    rest = lax.rem(live_count, 4)
    return lax.div(live_count + 1, 4), (rest == 1) | (rest == 2)


def by_core(core, mine, theirs, held):
    rows = mine.shape[0]
    held[pl.ds(pl.multiple_of(core * rows, rows), rows), :] = mine
    held[pl.ds(pl.multiple_of((1 - core) * rows, rows), rows), :] = theirs


def times_rows(grad, rows):
    return lax.dot_general(grad, rows, (((1,), (1,)), ((), ())), preferred_element_type=F32)


def near_gradient(top, ids_ref, own_ref, near_ref, dec_ref, part_ref, far_kept, grad, dec_near, near_sem, far_sem):
    blocks = near_sem.shape[0]
    kept, _, cut = far_kept.shape
    latent = lax.axis_index("latent")
    here = lax.div(latent & top, top)
    live_count = ids_ref[0, blocks]
    far_count = jnp.minimum(live_count, 4 * kept)

    def near_copy(n):
        quad, place = in_quads(n)
        return pltpu.make_async_copy(rows_of(dec_ref, ids_ref[0, n], here), dec_near.at[quad, place, :], near_sem.at[n])

    def far_copy(n):
        quad, place = in_quads(n)
        return pltpu.make_async_copy(rows_of(dec_ref, ids_ref[0, n], 1 - here), far_kept.at[quad, place, :], far_sem.at[n])

    lax.fori_loop(0, live_count, lambda n, c: (near_copy(n).start(), c)[1], 0)
    lax.fori_loop(0, far_count, lambda n, c: (far_copy(n).start(), c)[1], 0)
    by_core(latent & 1, own_ref[:, :cut], near_ref[:, :cut], grad)

    def multiply(quad, size):
        for n in [4 * quad + i for i in range(size)]:
            pl.when(n < live_count)(lambda n=n: near_copy(n).wait())
        places = pl.ds(0, size * BLOCK)
        part_ref[quad, :, places] = times_rows(grad[...], dec_near[quad, places, :])

    quads, last_pair = quads_of(live_count)
    lax.fori_loop(0, quads, lambda quad, c: (multiply(quad, 4), c)[1], 0)
    pl.when(last_pair)(lambda: multiply(quads, 2))
    lax.fori_loop(0, far_count, lambda n, c: (far_copy(n).wait(), c)[1], 0)


def code_gradient(
    top, ids_ref, own_ref, got_ref, far_ref, stay_ref, other_ref, part_ref, far_kept, dec_ref,
    out_ref, recon_ref, mean_ref, grad, fitted, dec_far, far_sem,
):
    blocks = far_sem.shape[0]
    kept, _, cut = far_kept.shape
    latent = lax.axis_index("latent")
    there = 1 - lax.div(latent & top, top)
    core = latent & 1
    live_count = ids_ref[0, blocks]

    def far_copy(n):
        quad, place = in_quads(n)
        return pltpu.make_async_copy(rows_of(dec_ref, ids_ref[0, n], there), dec_far.at[quad - kept, place, :], far_sem.at[n])

    lax.fori_loop(4 * kept, live_count, lambda n, c: (far_copy(n).start(), c)[1], 0)
    by_core(core, got_ref[:, :cut], far_ref[:, :cut], grad)
    out_ref[...] = jnp.zeros_like(out_ref)

    def multiply(quad, size, held, offset):
        blocks_here = [4 * quad + i for i in range(size)]
        if offset:
            for n in blocks_here:
                pl.when(n < live_count)(lambda n=n: far_copy(n).wait())
        places = pl.ds(0, size * BLOCK)
        product = (part_ref[quad, :, places] + times_rows(grad[...], held[quad - offset, places, :])).astype(BF16)
        for i, n in enumerate(blocks_here):

            @pl.when(n < live_count)
            def _(i=i, n=n):
                lanes = pl.ds(pl.multiple_of(ids_ref[0, n] * BLOCK, BLOCK), BLOCK)
                out_ref[:, lanes] = product[:, i * BLOCK : (i + 1) * BLOCK]

    quads, last_pair = quads_of(live_count)
    lax.fori_loop(0, jnp.minimum(quads, kept), lambda quad, c: (multiply(quad, 4, far_kept, 0), c)[1], 0)
    lax.fori_loop(kept, quads, lambda quad, c: (multiply(quad, 4, dec_far, kept), c)[1], 0)
    pl.when(last_pair & (quads < kept))(lambda: multiply(quads, 2, far_kept, 0))
    pl.when(last_pair & (quads >= kept))(lambda: multiply(quads, 2, dec_far, kept))
    columns = stay_ref.shape[1]
    by_core(core, stay_ref[...].astype(F32), other_ref[:, :columns].astype(F32), fitted)
    recon_ref[...] = jnp.transpose(fitted[...]).astype(BF16)
    squares = sum(ref[:, cut:].astype(F32) for ref in (own_ref, got_ref, far_ref)) + other_ref[:, columns:].astype(F32)
    total = jnp.sum(jnp.sum(squares, axis=0, keepdims=True), axis=1, keepdims=True)
    mean_ref[...] = total / (grad.shape[0] * 2 * cut)


def swap(value, axis, bit):
    size = lax.axis_size(axis)
    return lax.ppermute(value, axis, [(i, i ^ bit) for i in range(size)])


def in_hbm(value):
    return pltpu.with_memory_space_constraint(value, pltpu.HBM)


def part(value, start, size, axis):
    return lax.dynamic_slice_in_dim(value, start, size, axis)


def encode_call(block_list, block_count, x, bias, targets, gain, enc, dec, width):
    tok_rows, model_width = x.shape
    local_latents = enc.shape[1]
    blocks = local_latents // BLOCK
    quad_slots = (blocks + 3) // 4
    rows = tok_rows // 2
    vmem = pl.BlockSpec(memory_space=pltpu.VMEM)
    smem = pl.BlockSpec(memory_space=pltpu.SMEM)
    anyw = pl.BlockSpec(memory_space=pl.ANY)
    return pl.pallas_call(
        encode_decode,
        out_shape=(
            pltpu.VMEM((rows, model_width), F32),
            pltpu.VMEM((rows, model_width), BF16),
            pltpu.SMEM((1, blocks + 1), jnp.int32),
            pltpu.VMEM((rows + 16, width), BF16),
            pltpu.VMEM((1, width), F32),
        ),
        in_specs=[anyw, smem] + [anyw] * 6,
        out_specs=(vmem, vmem, smem, vmem, vmem),
        scratch_shapes=[
            pltpu.SMEM(block_list.shape, jnp.int32),
            pltpu.VMEM((tok_rows, model_width), BF16),
            pltpu.VMEM((1, local_latents), F32),
            pltpu.VMEM((rows, model_width), BF16),
            pltpu.VMEM((1, model_width), F32),
            pltpu.VMEM((quad_slots, model_width, 4 * BLOCK), BF16),
            pltpu.VMEM((quad_slots, 4 * BLOCK, model_width), BF16),
            pltpu.VMEM((quad_slots, tok_rows, 4 * BLOCK), BF16),
            pltpu.VMEM((tok_rows, model_width), F32),
            pltpu.SemaphoreType.DMA((5,)),
            pltpu.SemaphoreType.DMA((blocks,)),
            pltpu.SemaphoreType.DMA((blocks,)),
        ],
        compiler_params=pltpu.CompilerParams(vmem_limit_bytes=32 << 20),
        name="encode_decode",
    )(block_list, block_count, x, bias, targets, gain, enc, dec)


def local(residuals, targets, enc_weight, enc_bias, dec_weight, out_gain, block_list, block_count):
    tok_rows, model_width = residuals.shape[1:]
    local_latents = enc_weight.shape[2]
    blocks = local_latents // BLOCK
    slots = (blocks + 3) // 4
    kept = min(KEPT, slots)
    more = max(slots - kept, 1)
    quad = 4 * BLOCK
    layers, latents = lax.axis_size("layer"), lax.axis_size("latent")
    layer, latent = lax.axis_index("layer"), lax.axis_index("latent")
    core = latent % 2
    rows = tok_rows // 2
    chips = latents // 2
    width = model_width // chips
    column = (latent // 2) * width

    layer_bits = [1 << s for s in range((layers - 1).bit_length())]
    chip_bits = [1 << s for s in range((chips - 1).bit_length(), 0, -1)]

    dec_hbm = in_hbm(dec_weight[0])
    vmem = pl.BlockSpec(memory_space=pltpu.VMEM)
    smem = pl.BlockSpec(memory_space=pltpu.SMEM)
    anyw = pl.BlockSpec(memory_space=pl.ANY)
    keep, send, ids, beside, gain = encode_call(
        in_hbm(block_list), block_count, in_hbm(residuals[0]), in_hbm(enc_bias), in_hbm(targets[0]), in_hbm(out_gain),
        in_hbm(enc_weight[0]), dec_hbm, width,
    )

    held = keep + swap(send, "latent", 1).astype(F32)
    for bit in chip_bits:
        half = held.shape[1] // 2
        upper = (latent & bit) != 0
        away = jnp.where(upper, held[:, :half], held[:, half:]).astype(BF16)
        mine = jnp.where(upper, held[:, half:], held[:, :half])
        if bit == chip_bits[-1]:
            near_beside = swap(beside, "layer", 1)
        held = mine + swap(away, "latent", bit).astype(F32)
    own = held
    near = swap(own.astype(BF16), "layer", 1).astype(F32)
    target = beside[:rows]
    near_target = near_beside[:rows]
    near_gain = sum(near_beside[rows + i : rows + i + 1].astype(F32) for i in range(3))
    square = gain * gain
    near_square = near_gain * near_gain
    all_square = square + near_square

    low = (layer & 1) == 0

    def pair_sums(own, near):
        own_error = square * own - gain * target.astype(F32)
        near_error = near_square * near - near_gain * near_target.astype(F32)
        before = jnp.where(low, own, own + near)
        after = jnp.where(low, own_error + near_square * own + near_error, own_error + square * near)
        all_after = own_error + near_error + jnp.where(low, near_square * own, square * near)
        return before, after, own + near, all_after

    before, after, all_before, all_after = pair_sums(own, near)
    after_square = jnp.where(low, square + near_square, square)
    for step in layer_bits[1:]:
        upper = (layer & step) != 0
        there_square = swap(all_square, "layer", step)
        if step == layer_bits[-1]:
            outgoing = jnp.where((layer & step) == 0, all_before, all_after).astype(BF16)
            if len(layer_bits) == 2:
                own, near, outgoing = lax.optimization_barrier((own, near, outgoing))
                before, after, all_before, _ = pair_sums(own, near)
            got = swap(outgoing, "layer", step)
            break
        there_before = swap(all_before.astype(BF16), "layer", step).astype(F32)
        there_after = swap(all_after.astype(BF16), "layer", step).astype(F32)
        before, after = (
            jnp.where(upper, before + there_before, before),
            jnp.where(upper, after + after_square * there_before, after + there_square * all_before + there_after),
        )
        after_square = jnp.where(upper, after_square, after_square + there_square)
        all_before, all_after = (
            all_before + there_before,
            all_after + there_after + jnp.where(upper, all_square * there_before, there_square * all_before),
        )
        all_square = all_square + there_square

    columns = width // 2
    message, stay, send = pl.pallas_call(
        finish,
        out_shape=(
            pltpu.VMEM((rows, width + BLOCK), BF16),
            pltpu.VMEM((rows, columns), BF16),
            pltpu.VMEM((rows, columns), BF16),
        ),
        in_specs=[vmem] * 8,
        out_specs=(vmem, vmem, vmem),
        compiler_params=pltpu.CompilerParams(vmem_limit_bytes=16 << 20),
        name="finish",
    )(got, before, after, all_before, there_square, after_square, gain, beside)

    for bit in reversed(chip_bits[1:]):
        upper = (latent & bit) != 0
        got = swap(message, "latent", bit)
        cut = message.shape[1] - BLOCK
        here, there = message[:, :cut], got[:, :cut]
        squares = (message[:, cut:].astype(F32) + got[:, cut:].astype(F32)).astype(BF16)
        message = jnp.concatenate([jnp.where(upper, there, here), jnp.where(upper, here, there), squares], axis=1)
    top, cut = chip_bits[0], model_width // 2
    got = swap(message, "latent", top)
    near = swap(message[:, :cut], "latent", 1)
    send = jnp.concatenate([send, message[:, cut:]], axis=1)
    near_part, far_kept = pl.pallas_call(
        functools.partial(near_gradient, top),
        out_shape=(pltpu.VMEM((slots, tok_rows, quad), F32), pltpu.VMEM((kept, quad, cut), BF16)),
        in_specs=[smem, vmem, vmem, anyw],
        out_specs=(vmem, vmem),
        scratch_shapes=[
            pltpu.VMEM((tok_rows, cut), BF16),
            pltpu.VMEM((slots, quad, cut), BF16),
            pltpu.SemaphoreType.DMA((blocks,)),
            pltpu.SemaphoreType.DMA((blocks,)),
        ],
        compiler_params=pltpu.CompilerParams(vmem_limit_bytes=24 << 20),
        name="near_gradient",
    )(ids, message, near, dec_hbm)
    got, near_part, send = lax.optimization_barrier((got, near_part, send))
    far = swap(got, "latent", 1)
    other = swap(send, "latent", 1)

    code_grad, recon, loss = pl.pallas_call(
        functools.partial(code_gradient, top),
        out_shape=(
            jax.ShapeDtypeStruct((tok_rows, local_latents), BF16),
            jax.ShapeDtypeStruct((columns, tok_rows), BF16),
            jax.ShapeDtypeStruct((1, 1), F32),
        ),
        in_specs=[smem] + [vmem] * 7 + [anyw],
        out_specs=(vmem, vmem, vmem),
        scratch_shapes=[
            pltpu.VMEM((tok_rows, cut), BF16),
            pltpu.VMEM((tok_rows, columns), F32),
            pltpu.VMEM((more, quad, cut), BF16),
            pltpu.SemaphoreType.DMA((blocks,)),
        ],
        compiler_params=pltpu.CompilerParams(vmem_limit_bytes=16 << 20),
        name="code_gradient",
    )(ids, message, got, far, stay, other, *[pltpu.with_memory_space_constraint(a, pltpu.VMEM) for a in (near_part, far_kept)], dec_hbm)
    return recon.T[None], code_grad[None], loss


def solution(mesh):
    placed = (
        P("layer", "groups", None),
        P("layer", "groups", None),
        P("layer", None, "latent"),
        P("layer", "latent"),
        P("layer", "latent", None),
        P("layer", None),
        P("layer", "groups", None),
        P("layer", "groups"),
    )
    return jax.shard_map(
        local,
        mesh=mesh,
        in_specs=placed,
        out_specs=(
            P("layer", "groups", "latent"),
            P("layer", "groups", "latent"),
            P("groups", "layer"),
        ),
        check_vma=False,
    )
```

```python
import functools

import jax
import jax.numpy as jnp
from jax import lax
from jax.experimental import pallas as pl
from jax.experimental.pallas import tpu as pltpu
from jax.sharding import PartitionSpec as P

BLOCK = 128
PAIR = 2 * BLOCK
KEPT = 2
F32 = jnp.float32
BF16 = jnp.bfloat16


def encode_decode(
    top, list_any, count_ref, x_any, bias_any, target_any, gain_any, enc_ref, dec_ref,
    keep_ref, send_ref, ids_ref, beside_ref, own_gain_ref,
    list_ref, x_ref, bias_ref, target_ref, gain_ref, enc_held, dec_held, codes, total, in_sem, enc_sem, dec_sem,
):
    blocks = enc_ref.shape[1] // BLOCK
    list_load = pltpu.make_async_copy(list_any, list_ref, in_sem.at[0])
    list_load.start()
    where = lax.axis_index("latent")
    first = where * blocks
    core = lax.rem(where, 2)
    rows = keep_ref.shape[0]
    mine = pl.ds(pl.multiple_of(core * rows, rows), rows)
    loads = [
        pltpu.make_async_copy(x_any, x_ref, in_sem.at[1]),
        pltpu.make_async_copy(bias_any, bias_ref, in_sem.at[2]),
        pltpu.make_async_copy(target_any.at[mine, :], target_ref, in_sem.at[3]),
        pltpu.make_async_copy(gain_any, gain_ref, in_sem.at[4]),
    ]
    for load in loads:
        load.start()
    total[...] = jnp.zeros_like(total)

    def place_of(n):
        return lax.div(n, 4), pl.ds(pl.multiple_of(lax.rem(n, 4) * BLOCK, BLOCK), BLOCK)

    def rows_of(n):
        return pl.ds(pl.multiple_of(ids_ref[0, n] * BLOCK, BLOCK), BLOCK)

    def enc_copy(n):
        quad, place = place_of(n)
        return pltpu.make_async_copy(enc_ref.at[:, rows_of(n)], enc_held.at[quad, :, place], enc_sem.at[n])

    def dec_copy(n):
        quad, place = place_of(n)
        return pltpu.make_async_copy(dec_ref.at[rows_of(n), :], dec_held.at[quad, place, :], dec_sem.at[n])

    list_load.wait()
    count = count_ref[0, 0]

    def look(slot, n):
        block = list_ref[0, 0, slot] - first
        live = (slot < count) & (block >= 0) & (block < blocks)

        @pl.when(live)
        def _():
            ids_ref[0, n] = block
            enc_copy(n).start()

        return n + live.astype(jnp.int32)

    live_count = lax.fori_loop(0, jnp.minimum(count, list_ref.shape[2]), look, jnp.int32(0))
    ids_ref[0, blocks] = live_count
    lax.fori_loop(0, live_count, lambda n, c: (dec_copy(n).start(), c)[1], 0)
    quads = lax.div(live_count + 1, 4)
    last_pair = (lax.rem(live_count, 4) == 1) | (lax.rem(live_count, 4) == 2)

    def clear(n, carry):
        quad, place = place_of(n)
        dec_held[quad, place, :] = jnp.zeros((BLOCK, dec_held.shape[2]), BF16)
        ids_ref[0, n] = ids_ref[0, 0]
        return carry

    lax.fori_loop(live_count, jnp.where(last_pair, 4 * quads + 2, 4 * quads), clear, 0)
    for load in loads:
        load.wait()

    width = own_gain_ref.shape[1]
    for chip in range(target_ref.shape[1] // width):

        @pl.when(lax.div(where, 2) == chip)
        def _(columns=slice(chip * width, (chip + 1) * width)):
            beside_ref[:rows, :] = target_ref[:, columns]
            own_gain_ref[...] = gain_ref[:, columns]

    left, terms = own_gain_ref[...], []
    for _ in range(3):
        terms.append(left.astype(BF16).astype(F32))
        left = left - terms[-1]
    row = lax.broadcasted_iota(jnp.int32, (beside_ref.shape[0] - rows, width), 0)
    beside_ref[rows:, :] = sum(jnp.where(row == i, term, 0.0) for i, term in enumerate(terms)).astype(BF16)

    def encode(n, size):
        for i in range(size):
            pl.when(n + i < live_count)(lambda i=i: enc_copy(n + i).wait())
        quad = lax.div(n, 4)
        lanes = pl.ds(pl.multiple_of(lax.rem(n, 4) * BLOCK, size * BLOCK), size * BLOCK)
        bias = jnp.concatenate([bias_ref[:, rows_of(n + i)] for i in range(size)], axis=1)
        pre_act = jnp.dot(x_ref[...], enc_held[quad, :, lanes], preferred_element_type=F32) + bias
        lane = lax.broadcasted_iota(jnp.int32, pre_act.shape, 1)
        used = lane < (live_count - n) * BLOCK
        codes[quad, :, lanes] = jnp.where(used, jnp.maximum(pre_act, 0.0), 0.0).astype(BF16)

    def decode(pair, carry):
        quad, lanes = lax.div(pair, 2), pl.ds(pl.multiple_of(lax.rem(pair, 2) * PAIR, PAIR), PAIR)
        for n in (2 * pair, 2 * pair + 1):
            pl.when(n < live_count)(lambda n=n: dec_copy(n).wait())
        total[...] += jnp.dot(codes[quad, :, lanes], dec_held[quad, lanes, :], preferred_element_type=F32)
        return carry

    pairs = lax.div(live_count + 1, 2)
    fours = jnp.where(live_count <= 4, 0, quads)
    lax.fori_loop(0, fours, lambda quad, c: (encode(4 * quad, 4), c)[1], 0)
    lax.fori_loop(2 * fours, pairs, lambda pair, c: (encode(2 * pair, 2), c)[1], 0)
    lax.fori_loop(0, pairs, decode, 0)

    theirs = pl.ds(pl.multiple_of((1 - core) * rows, rows), rows)
    cut = keep_ref.shape[1] // 2
    here = lax.div(where & top, top)
    for place, half in ((0, 1 - here), (1, here)):
        columns = pl.ds(pl.multiple_of(half * cut, cut), cut)
        keep_ref[:, place * cut : (place + 1) * cut] = total[mine, columns]
        send_ref[:, place * cut : (place + 1) * cut] = total[theirs, columns].astype(BF16)


def finish(
    got_ref, before_ref, after_ref, all_ref, there_square_ref, after_square_ref, gain_ref, target_ref,
    message_ref, stay_ref, send_ref,
):
    got = got_ref[...].astype(F32)
    width = got.shape[1]
    low = (lax.axis_index("layer") & (lax.axis_size("layer") // 2)) == 0
    fitted = gain_ref[...] * jnp.where(low, before_ref[...], before_ref[...] + got)
    error_term = fitted - target_ref[: got.shape[0], :].astype(F32)
    squares = error_term * error_term
    added = functools.reduce(add_terms, [squares[:, i : i + BLOCK] for i in range(0, width - BLOCK + 1, BLOCK)])
    rest = width % BLOCK
    if rest:
        zeros = jnp.zeros((squares.shape[0], BLOCK - rest), F32)
        added = added + jnp.concatenate([squares[:, width - rest :], zeros], axis=1)
    entering = jnp.where(low, there_square_ref[...] * all_ref[...] + got, after_square_ref[...] * got)
    message_ref[:, :width] = (after_ref[...] + entering).astype(BF16)
    message_ref[:, width:] = added.astype(BF16)
    left, right = fitted[:, : width // 2].astype(BF16), fitted[:, width // 2 :].astype(BF16)
    first = (lax.axis_index("latent") & 1) == 0
    stay_ref[...] = jnp.where(first, left, right)
    send_ref[...] = jnp.where(first, right, left)


def add_terms(one, two):
    return one + two


def rows_of(dec_ref, block, half):
    cut = dec_ref.shape[1] // 2
    return dec_ref.at[pl.ds(pl.multiple_of(block * BLOCK, BLOCK), BLOCK), pl.ds(pl.multiple_of(half * cut, cut), cut)]


def in_quads(n):
    return lax.div(n, 4), pl.ds(pl.multiple_of(lax.rem(n, 4) * BLOCK, BLOCK), BLOCK)


def quads_of(live_count):
    rest = lax.rem(live_count, 4)
    return lax.div(live_count + 1, 4), (rest == 1) | (rest == 2)


def by_core(core, mine, theirs, held):
    rows = mine.shape[0]
    held[pl.ds(pl.multiple_of(core * rows, rows), rows), :] = mine
    held[pl.ds(pl.multiple_of((1 - core) * rows, rows), rows), :] = theirs


def times_rows(grad, rows):
    return lax.dot_general(grad, rows, (((1,), (1,)), ((), ())), preferred_element_type=F32)


def near_gradient(top, ids_ref, own_ref, near_ref, dec_ref, part_ref, far_kept, grad, dec_near, near_sem, far_sem):
    blocks = near_sem.shape[0]
    kept, _, cut = far_kept.shape
    latent = lax.axis_index("latent")
    here = lax.div(latent & top, top)
    live_count = ids_ref[0, blocks]
    far_count = jnp.minimum(live_count, 4 * kept)

    def near_copy(n):
        quad, place = in_quads(n)
        return pltpu.make_async_copy(rows_of(dec_ref, ids_ref[0, n], here), dec_near.at[quad, place, :], near_sem.at[n])

    def far_copy(n):
        quad, place = in_quads(n)
        return pltpu.make_async_copy(rows_of(dec_ref, ids_ref[0, n], 1 - here), far_kept.at[quad, place, :], far_sem.at[n])

    lax.fori_loop(0, live_count, lambda n, c: (near_copy(n).start(), c)[1], 0)
    lax.fori_loop(0, far_count, lambda n, c: (far_copy(n).start(), c)[1], 0)
    by_core(latent & 1, own_ref[:, :cut], near_ref[:, :cut], grad)

    def multiply(quad, size):
        for n in [4 * quad + i for i in range(size)]:
            pl.when(n < live_count)(lambda n=n: near_copy(n).wait())
        places = pl.ds(0, size * BLOCK)
        part_ref[quad, :, places] = times_rows(grad[...], dec_near[quad, places, :])

    quads, last_pair = quads_of(live_count)
    lax.fori_loop(0, quads, lambda quad, c: (multiply(quad, 4), c)[1], 0)
    pl.when(last_pair)(lambda: multiply(quads, 2))
    lax.fori_loop(0, far_count, lambda n, c: (far_copy(n).wait(), c)[1], 0)


def code_gradient(
    top, ids_ref, own_ref, got_ref, far_ref, stay_ref, other_ref, part_ref, far_kept, dec_ref,
    out_ref, recon_ref, mean_ref, grad, fitted, dec_far, far_sem,
):
    blocks = far_sem.shape[0]
    kept, _, cut = far_kept.shape
    latent = lax.axis_index("latent")
    there = 1 - lax.div(latent & top, top)
    core = latent & 1
    live_count = ids_ref[0, blocks]

    def far_copy(n):
        quad, place = in_quads(n)
        return pltpu.make_async_copy(rows_of(dec_ref, ids_ref[0, n], there), dec_far.at[quad - kept, place, :], far_sem.at[n])

    lax.fori_loop(4 * kept, live_count, lambda n, c: (far_copy(n).start(), c)[1], 0)
    by_core(core, got_ref[:, :cut], far_ref[:, :cut], grad)
    out_ref[...] = jnp.zeros_like(out_ref)

    def multiply(quad, size, held, offset):
        blocks_here = [4 * quad + i for i in range(size)]
        if offset:
            for n in blocks_here:
                pl.when(n < live_count)(lambda n=n: far_copy(n).wait())
        places = pl.ds(0, size * BLOCK)
        product = (part_ref[quad, :, places] + times_rows(grad[...], held[quad - offset, places, :])).astype(BF16)
        for i, n in enumerate(blocks_here):

            @pl.when(n < live_count)
            def _(i=i, n=n):
                lanes = pl.ds(pl.multiple_of(ids_ref[0, n] * BLOCK, BLOCK), BLOCK)
                out_ref[:, lanes] = product[:, i * BLOCK : (i + 1) * BLOCK]

    quads, last_pair = quads_of(live_count)
    lax.fori_loop(0, jnp.minimum(quads, kept), lambda quad, c: (multiply(quad, 4, far_kept, 0), c)[1], 0)
    lax.fori_loop(kept, quads, lambda quad, c: (multiply(quad, 4, dec_far, kept), c)[1], 0)
    pl.when(last_pair & (quads < kept))(lambda: multiply(quads, 2, far_kept, 0))
    pl.when(last_pair & (quads >= kept))(lambda: multiply(quads, 2, dec_far, kept))
    columns = stay_ref.shape[1]
    by_core(core, stay_ref[...].astype(F32), other_ref[:, :columns].astype(F32), fitted)
    recon_ref[...] = jnp.transpose(fitted[...]).astype(BF16)
    squares = sum(ref[:, cut:].astype(F32) for ref in (own_ref, got_ref, far_ref)) + other_ref[:, columns:].astype(F32)
    total = jnp.sum(jnp.sum(squares, axis=0, keepdims=True), axis=1, keepdims=True)
    mean_ref[...] = total / (grad.shape[0] * 2 * cut)


def swap(value, axis, bit):
    size = lax.axis_size(axis)
    return lax.ppermute(value, axis, [(i, i ^ bit) for i in range(size)])


def in_hbm(value):
    return pltpu.with_memory_space_constraint(value, pltpu.HBM)


def part(value, start, size, axis):
    return lax.dynamic_slice_in_dim(value, start, size, axis)


def encode_call(top, block_list, block_count, x, bias, targets, gain, enc, dec, width):
    tok_rows, model_width = x.shape
    local_latents = enc.shape[1]
    blocks = local_latents // BLOCK
    quad_slots = (blocks + 3) // 4
    rows = tok_rows // 2
    vmem = pl.BlockSpec(memory_space=pltpu.VMEM)
    smem = pl.BlockSpec(memory_space=pltpu.SMEM)
    anyw = pl.BlockSpec(memory_space=pl.ANY)
    return pl.pallas_call(
        functools.partial(encode_decode, top),
        out_shape=(
            pltpu.VMEM((rows, model_width), F32),
            pltpu.VMEM((rows, model_width), BF16),
            pltpu.SMEM((1, blocks + 1), jnp.int32),
            pltpu.VMEM((rows + 16, width), BF16),
            pltpu.VMEM((1, width), F32),
        ),
        in_specs=[anyw, smem] + [anyw] * 6,
        out_specs=(vmem, vmem, smem, vmem, vmem),
        scratch_shapes=[
            pltpu.SMEM(block_list.shape, jnp.int32),
            pltpu.VMEM((tok_rows, model_width), BF16),
            pltpu.VMEM((1, local_latents), F32),
            pltpu.VMEM((rows, model_width), BF16),
            pltpu.VMEM((1, model_width), F32),
            pltpu.VMEM((quad_slots, model_width, 4 * BLOCK), BF16),
            pltpu.VMEM((quad_slots, 4 * BLOCK, model_width), BF16),
            pltpu.VMEM((quad_slots, tok_rows, 4 * BLOCK), BF16),
            pltpu.VMEM((tok_rows, model_width), F32),
            pltpu.SemaphoreType.DMA((5,)),
            pltpu.SemaphoreType.DMA((blocks,)),
            pltpu.SemaphoreType.DMA((blocks,)),
        ],
        compiler_params=pltpu.CompilerParams(vmem_limit_bytes=32 << 20),
        name="encode_decode",
    )(block_list, block_count, x, bias, targets, gain, enc, dec)


def local(residuals, targets, enc_weight, enc_bias, dec_weight, out_gain, block_list, block_count):
    tok_rows, model_width = residuals.shape[1:]
    local_latents = enc_weight.shape[2]
    blocks = local_latents // BLOCK
    slots = (blocks + 3) // 4
    kept = min(KEPT, slots)
    more = max(slots - kept, 1)
    quad = 4 * BLOCK
    layers, latents = lax.axis_size("layer"), lax.axis_size("latent")
    layer, latent = lax.axis_index("layer"), lax.axis_index("latent")
    core = latent % 2
    rows = tok_rows // 2
    chips = latents // 2
    width = model_width // chips
    column = (latent // 2) * width

    layer_bits = [1 << s for s in range((layers - 1).bit_length())]
    chip_bits = [1 << s for s in range((chips - 1).bit_length(), 0, -1)]

    dec_hbm = in_hbm(dec_weight[0])
    vmem = pl.BlockSpec(memory_space=pltpu.VMEM)
    smem = pl.BlockSpec(memory_space=pltpu.SMEM)
    anyw = pl.BlockSpec(memory_space=pl.ANY)
    keep, send, ids, beside, gain = encode_call(
        chip_bits[0], in_hbm(block_list), block_count, in_hbm(residuals[0]), in_hbm(enc_bias), in_hbm(targets[0]), in_hbm(out_gain),
        in_hbm(enc_weight[0]), dec_hbm, width,
    )

    cut = model_width // 2
    got = swap(send, "latent", 1)
    away = (keep[:, :cut] + got[:, :cut].astype(F32)).astype(BF16)
    near_beside = swap(beside, "layer", 1)
    keep, got, away = lax.optimization_barrier((keep, got, away))
    held = keep[:, cut:] + got[:, cut:].astype(F32) + swap(away, "latent", chip_bits[0]).astype(F32)
    for bit in chip_bits[1:]:
        half = held.shape[1] // 2
        upper = (latent & bit) != 0
        away = jnp.where(upper, held[:, :half], held[:, half:]).astype(BF16)
        mine = jnp.where(upper, held[:, half:], held[:, :half])
        held = mine + swap(away, "latent", bit).astype(F32)
    own = held
    near = swap(own.astype(BF16), "layer", 1).astype(F32)
    target = beside[:rows]
    near_target = near_beside[:rows]
    near_gain = sum(near_beside[rows + i : rows + i + 1].astype(F32) for i in range(3))
    square = gain * gain
    near_square = near_gain * near_gain
    all_square = square + near_square

    low = (layer & 1) == 0

    def pair_sums(own, near):
        own_error = square * own - gain * target.astype(F32)
        near_error = near_square * near - near_gain * near_target.astype(F32)
        before = jnp.where(low, own, own + near)
        after = jnp.where(low, own_error + near_square * own + near_error, own_error + square * near)
        all_after = own_error + near_error + jnp.where(low, near_square * own, square * near)
        return before, after, own + near, all_after

    before, after, all_before, all_after = pair_sums(own, near)
    after_square = jnp.where(low, square + near_square, square)
    for step in layer_bits[1:]:
        upper = (layer & step) != 0
        there_square = swap(all_square, "layer", step)
        if step == layer_bits[-1]:
            outgoing = jnp.where((layer & step) == 0, all_before, all_after).astype(BF16)
            if len(layer_bits) == 2:
                own, near, outgoing = lax.optimization_barrier((own, near, outgoing))
                before, after, all_before, _ = pair_sums(own, near)
            got = swap(outgoing, "layer", step)
            break
        there_before = swap(all_before.astype(BF16), "layer", step).astype(F32)
        there_after = swap(all_after.astype(BF16), "layer", step).astype(F32)
        before, after = (
            jnp.where(upper, before + there_before, before),
            jnp.where(upper, after + after_square * there_before, after + there_square * all_before + there_after),
        )
        after_square = jnp.where(upper, after_square, after_square + there_square)
        all_before, all_after = (
            all_before + there_before,
            all_after + there_after + jnp.where(upper, all_square * there_before, there_square * all_before),
        )
        all_square = all_square + there_square

    columns = width // 2
    message, stay, send = pl.pallas_call(
        finish,
        out_shape=(
            pltpu.VMEM((rows, width + BLOCK), BF16),
            pltpu.VMEM((rows, columns), BF16),
            pltpu.VMEM((rows, columns), BF16),
        ),
        in_specs=[vmem] * 8,
        out_specs=(vmem, vmem, vmem),
        compiler_params=pltpu.CompilerParams(vmem_limit_bytes=16 << 20),
        name="finish",
    )(got, before, after, all_before, there_square, after_square, gain, beside)

    for bit in reversed(chip_bits[1:]):
        upper = (latent & bit) != 0
        got = swap(message, "latent", bit)
        cut = message.shape[1] - BLOCK
        here, there = message[:, :cut], got[:, :cut]
        squares = (message[:, cut:].astype(F32) + got[:, cut:].astype(F32)).astype(BF16)
        message = jnp.concatenate([jnp.where(upper, there, here), jnp.where(upper, here, there), squares], axis=1)
    top, cut = chip_bits[0], model_width // 2
    got = swap(message, "latent", top)
    near = swap(message[:, :cut], "latent", 1)
    send = jnp.concatenate([send, message[:, cut:]], axis=1)
    near_part, far_kept = pl.pallas_call(
        functools.partial(near_gradient, top),
        out_shape=(pltpu.VMEM((slots, tok_rows, quad), F32), pltpu.VMEM((kept, quad, cut), BF16)),
        in_specs=[smem, vmem, vmem, anyw],
        out_specs=(vmem, vmem),
        scratch_shapes=[
            pltpu.VMEM((tok_rows, cut), BF16),
            pltpu.VMEM((slots, quad, cut), BF16),
            pltpu.SemaphoreType.DMA((blocks,)),
            pltpu.SemaphoreType.DMA((blocks,)),
        ],
        compiler_params=pltpu.CompilerParams(vmem_limit_bytes=24 << 20),
        name="near_gradient",
    )(ids, message, near, dec_hbm)
    got, near_part, send = lax.optimization_barrier((got, near_part, send))
    far = swap(got, "latent", 1)
    other = swap(send, "latent", 1)

    code_grad, recon, loss = pl.pallas_call(
        functools.partial(code_gradient, top),
        out_shape=(
            jax.ShapeDtypeStruct((tok_rows, local_latents), BF16),
            jax.ShapeDtypeStruct((columns, tok_rows), BF16),
            jax.ShapeDtypeStruct((1, 1), F32),
        ),
        in_specs=[smem] + [vmem] * 7 + [anyw],
        out_specs=(vmem, vmem, vmem),
        scratch_shapes=[
            pltpu.VMEM((tok_rows, cut), BF16),
            pltpu.VMEM((tok_rows, columns), F32),
            pltpu.VMEM((more, quad, cut), BF16),
            pltpu.SemaphoreType.DMA((blocks,)),
        ],
        compiler_params=pltpu.CompilerParams(vmem_limit_bytes=16 << 20),
        name="code_gradient",
    )(ids, message, got, far, stay, other, *[pltpu.with_memory_space_constraint(a, pltpu.VMEM) for a in (near_part, far_kept)], dec_hbm)
    return recon.T[None], code_grad[None], loss


def solution(mesh):
    placed = (
        P("layer", "groups", None),
        P("layer", "groups", None),
        P("layer", None, "latent"),
        P("layer", "latent"),
        P("layer", "latent", None),
        P("layer", None),
        P("layer", "groups", None),
        P("layer", "groups"),
    )
    return jax.shard_map(
        local,
        mesh=mesh,
        in_specs=placed,
        out_specs=(
            P("layer", "groups", "latent"),
            P("layer", "groups", "latent"),
            P("groups", "layer"),
        ),
        check_vma=False,
    )
```

```python
import functools

import jax
import jax.numpy as jnp
from jax import lax
from jax.experimental import pallas as pl
from jax.experimental.pallas import tpu as pltpu
from jax.sharding import PartitionSpec as P

BLOCK = 128
PAIR = 2 * BLOCK
KEPT = 2
F32 = jnp.float32
BF16 = jnp.bfloat16


def encode_decode(
    top, list_any, count_ref, x_any, bias_any, target_any, gain_any, enc_ref, dec_ref,
    keep_ref, send_ref, ids_ref, beside_ref, own_gain_ref,
    list_ref, x_ref, bias_ref, target_ref, gain_ref, enc_held, dec_held, codes, total, in_sem, enc_sem, dec_sem,
):
    blocks = enc_ref.shape[1] // BLOCK
    list_load = pltpu.make_async_copy(list_any, list_ref, in_sem.at[0])
    list_load.start()
    where = lax.axis_index("latent")
    first = where * blocks
    core = lax.rem(where, 2)
    rows = keep_ref.shape[0]
    mine = pl.ds(pl.multiple_of(core * rows, rows), rows)
    loads = [
        pltpu.make_async_copy(x_any, x_ref, in_sem.at[1]),
        pltpu.make_async_copy(bias_any, bias_ref, in_sem.at[2]),
        pltpu.make_async_copy(target_any.at[mine, :], target_ref, in_sem.at[3]),
        pltpu.make_async_copy(gain_any, gain_ref, in_sem.at[4]),
    ]
    for load in loads:
        load.start()
    total[...] = jnp.zeros_like(total)

    def place_of(n):
        return lax.div(n, 4), pl.ds(pl.multiple_of(lax.rem(n, 4) * BLOCK, BLOCK), BLOCK)

    def rows_of(n):
        return pl.ds(pl.multiple_of(ids_ref[0, n] * BLOCK, BLOCK), BLOCK)

    def enc_copy(n):
        quad, place = place_of(n)
        return pltpu.make_async_copy(enc_ref.at[:, rows_of(n)], enc_held.at[quad, :, place], enc_sem.at[n])

    def dec_copy(n):
        quad, place = place_of(n)
        return pltpu.make_async_copy(dec_ref.at[rows_of(n), :], dec_held.at[quad, place, :], dec_sem.at[n])

    list_load.wait()
    count = count_ref[0, 0]

    def look(slot, n):
        block = list_ref[0, 0, slot] - first
        live = (slot < count) & (block >= 0) & (block < blocks)

        @pl.when(live)
        def _():
            ids_ref[0, n] = block
            enc_copy(n).start()

        return n + live.astype(jnp.int32)

    live_count = lax.fori_loop(0, jnp.minimum(count, list_ref.shape[2]), look, jnp.int32(0))
    ids_ref[0, blocks] = live_count
    lax.fori_loop(0, live_count, lambda n, c: (dec_copy(n).start(), c)[1], 0)
    quads = lax.div(live_count + 1, 4)
    last_pair = (lax.rem(live_count, 4) == 1) | (lax.rem(live_count, 4) == 2)

    def clear(n, carry):
        quad, place = place_of(n)
        dec_held[quad, place, :] = jnp.zeros((BLOCK, dec_held.shape[2]), BF16)
        ids_ref[0, n] = ids_ref[0, 0]
        return carry

    lax.fori_loop(live_count, jnp.where(last_pair, 4 * quads + 2, 4 * quads), clear, 0)
    for load in loads:
        load.wait()

    width = own_gain_ref.shape[1]
    for chip in range(target_ref.shape[1] // width):

        @pl.when(lax.div(where, 2) == chip)
        def _(columns=slice(chip * width, (chip + 1) * width)):
            beside_ref[:rows, :] = target_ref[:, columns]
            own_gain_ref[...] = gain_ref[:, columns]

    left, terms = own_gain_ref[...], []
    for _ in range(3):
        terms.append(left.astype(BF16).astype(F32))
        left = left - terms[-1]
    row = lax.broadcasted_iota(jnp.int32, (beside_ref.shape[0] - rows, width), 0)
    beside_ref[rows:, :] = sum(jnp.where(row == i, term, 0.0) for i, term in enumerate(terms)).astype(BF16)

    def encode(n, size):
        for i in range(size):
            pl.when(n + i < live_count)(lambda i=i: enc_copy(n + i).wait())
        quad = lax.div(n, 4)
        lanes = pl.ds(pl.multiple_of(lax.rem(n, 4) * BLOCK, size * BLOCK), size * BLOCK)
        bias = jnp.concatenate([bias_ref[:, rows_of(n + i)] for i in range(size)], axis=1)
        pre_act = jnp.dot(x_ref[...], enc_held[quad, :, lanes], preferred_element_type=F32) + bias
        lane = lax.broadcasted_iota(jnp.int32, pre_act.shape, 1)
        used = lane < (live_count - n) * BLOCK
        codes[quad, :, lanes] = jnp.where(used, jnp.maximum(pre_act, 0.0), 0.0).astype(BF16)

    def decode(pair, carry):
        quad, lanes = lax.div(pair, 2), pl.ds(pl.multiple_of(lax.rem(pair, 2) * PAIR, PAIR), PAIR)
        for n in (2 * pair, 2 * pair + 1):
            pl.when(n < live_count)(lambda n=n: dec_copy(n).wait())
        total[...] += jnp.dot(codes[quad, :, lanes], dec_held[quad, lanes, :], preferred_element_type=F32)
        return carry

    pairs = lax.div(live_count + 1, 2)
    fours = jnp.where(live_count <= 4, 0, quads)
    lax.fori_loop(0, fours, lambda quad, c: (encode(4 * quad, 4), c)[1], 0)
    lax.fori_loop(2 * fours, pairs, lambda pair, c: (encode(2 * pair, 2), c)[1], 0)
    lax.fori_loop(0, pairs, decode, 0)

    theirs = pl.ds(pl.multiple_of((1 - core) * rows, rows), rows)
    cut = keep_ref.shape[1] // 2
    here = lax.div(where & top, top)
    for place, half in ((0, 1 - here), (1, here)):
        columns = pl.ds(pl.multiple_of(half * cut, cut), cut)
        keep_ref[:, place * cut : (place + 1) * cut] = total[mine, columns]
        send_ref[:, place * cut : (place + 1) * cut] = total[theirs, columns].astype(BF16)


def finish(
    got_ref, before_ref, after_ref, all_ref, there_square_ref, after_square_ref, gain_ref, target_ref,
    message_ref, stay_ref, send_ref,
):
    got = got_ref[...].astype(F32)
    width = got.shape[1]
    low = (lax.axis_index("layer") & (lax.axis_size("layer") // 2)) == 0
    fitted = gain_ref[...] * jnp.where(low, before_ref[...], before_ref[...] + got)
    error_term = fitted - target_ref[: got.shape[0], :].astype(F32)
    squares = error_term * error_term
    added = functools.reduce(add_terms, [squares[:, i : i + BLOCK] for i in range(0, width - BLOCK + 1, BLOCK)])
    rest = width % BLOCK
    if rest:
        zeros = jnp.zeros((squares.shape[0], BLOCK - rest), F32)
        added = added + jnp.concatenate([squares[:, width - rest :], zeros], axis=1)
    entering = jnp.where(low, there_square_ref[...] * all_ref[...] + got, after_square_ref[...] * got)
    message_ref[:, :width] = (after_ref[...] + entering).astype(BF16)
    message_ref[:, width:] = added.astype(BF16)
    left, right = fitted[:, : width // 2].astype(BF16), fitted[:, width // 2 :].astype(BF16)
    first = (lax.axis_index("latent") & 1) == 0
    stay_ref[...] = jnp.where(first, left, right)
    send_ref[...] = jnp.where(first, right, left)


def add_terms(one, two):
    return one + two


def rows_of(dec_ref, block, half):
    cut = dec_ref.shape[1] // 2
    return dec_ref.at[pl.ds(pl.multiple_of(block * BLOCK, BLOCK), BLOCK), pl.ds(pl.multiple_of(half * cut, cut), cut)]


def in_quads(n):
    return lax.div(n, 4), pl.ds(pl.multiple_of(lax.rem(n, 4) * BLOCK, BLOCK), BLOCK)


def quads_of(live_count):
    rest = lax.rem(live_count, 4)
    return lax.div(live_count + 1, 4), (rest == 1) | (rest == 2)


def by_core(core, mine, theirs, held):
    rows = mine.shape[0]
    held[pl.ds(pl.multiple_of(core * rows, rows), rows), :] = mine
    held[pl.ds(pl.multiple_of((1 - core) * rows, rows), rows), :] = theirs


def times_rows(grad, rows):
    return lax.dot_general(grad, rows, (((1,), (1,)), ((), ())), preferred_element_type=F32)


def near_gradient(top, ids_ref, own_ref, near_ref, dec_ref, part_ref, far_kept, grad, dec_near, near_sem, far_sem):
    blocks = near_sem.shape[0]
    kept, _, cut = far_kept.shape
    latent = lax.axis_index("latent")
    here = lax.div(latent & top, top)
    live_count = ids_ref[0, blocks]
    far_count = jnp.minimum(live_count, 4 * kept)

    def near_copy(n):
        quad, place = in_quads(n)
        return pltpu.make_async_copy(rows_of(dec_ref, ids_ref[0, n], here), dec_near.at[quad, place, :], near_sem.at[n])

    def far_copy(n):
        quad, place = in_quads(n)
        return pltpu.make_async_copy(rows_of(dec_ref, ids_ref[0, n], 1 - here), far_kept.at[quad, place, :], far_sem.at[n])

    lax.fori_loop(0, live_count, lambda n, c: (near_copy(n).start(), c)[1], 0)
    lax.fori_loop(0, far_count, lambda n, c: (far_copy(n).start(), c)[1], 0)
    by_core(latent & 1, own_ref[:, :cut], near_ref[:, :cut], grad)

    def multiply(quad, size):
        for n in [4 * quad + i for i in range(size)]:
            pl.when(n < live_count)(lambda n=n: near_copy(n).wait())
        places = pl.ds(0, size * BLOCK)
        part_ref[quad, :, places] = times_rows(grad[...], dec_near[quad, places, :])

    quads, last_pair = quads_of(live_count)
    lax.fori_loop(0, quads, lambda quad, c: (multiply(quad, 4), c)[1], 0)
    pl.when(last_pair)(lambda: multiply(quads, 2))
    lax.fori_loop(0, far_count, lambda n, c: (far_copy(n).wait(), c)[1], 0)


def code_gradient(
    top, ids_ref, own_ref, got_ref, far_ref, stay_ref, other_ref, part_ref, far_kept, dec_ref,
    out_ref, recon_ref, mean_ref, grad, fitted, dec_far, far_sem,
):
    blocks = far_sem.shape[0]
    kept, _, cut = far_kept.shape
    latent = lax.axis_index("latent")
    there = 1 - lax.div(latent & top, top)
    core = latent & 1
    live_count = ids_ref[0, blocks]

    def far_copy(n):
        quad, place = in_quads(n)
        return pltpu.make_async_copy(rows_of(dec_ref, ids_ref[0, n], there), dec_far.at[quad - kept, place, :], far_sem.at[n])

    lax.fori_loop(4 * kept, live_count, lambda n, c: (far_copy(n).start(), c)[1], 0)
    by_core(core, got_ref[:, :cut], far_ref[:, :cut], grad)
    out_ref[...] = jnp.zeros_like(out_ref)

    def multiply(quad, size, held, offset):
        blocks_here = [4 * quad + i for i in range(size)]
        if offset:
            for n in blocks_here:
                pl.when(n < live_count)(lambda n=n: far_copy(n).wait())
        places = pl.ds(0, size * BLOCK)
        product = (part_ref[quad, :, places] + times_rows(grad[...], held[quad - offset, places, :])).astype(BF16)
        for i, n in enumerate(blocks_here):

            @pl.when(n < live_count)
            def _(i=i, n=n):
                lanes = pl.ds(pl.multiple_of(ids_ref[0, n] * BLOCK, BLOCK), BLOCK)
                out_ref[:, lanes] = product[:, i * BLOCK : (i + 1) * BLOCK]

    quads, last_pair = quads_of(live_count)
    lax.fori_loop(0, jnp.minimum(quads, kept), lambda quad, c: (multiply(quad, 4, far_kept, 0), c)[1], 0)
    lax.fori_loop(kept, quads, lambda quad, c: (multiply(quad, 4, dec_far, kept), c)[1], 0)
    pl.when(last_pair & (quads < kept))(lambda: multiply(quads, 2, far_kept, 0))
    pl.when(last_pair & (quads >= kept))(lambda: multiply(quads, 2, dec_far, kept))
    columns = stay_ref.shape[1]
    by_core(core, stay_ref[...].astype(F32), other_ref[:, :columns].astype(F32), fitted)
    recon_ref[...] = jnp.transpose(fitted[...]).astype(BF16)
    squares = sum(ref[:, cut:].astype(F32) for ref in (own_ref, got_ref, far_ref)) + other_ref[:, columns:].astype(F32)
    total = jnp.sum(jnp.sum(squares, axis=0, keepdims=True), axis=1, keepdims=True)
    mean_ref[...] = total / (grad.shape[0] * 2 * cut)


def swap(value, axis, bit):
    size = lax.axis_size(axis)
    return lax.ppermute(value, axis, [(i, i ^ bit) for i in range(size)])


def in_hbm(value):
    return pltpu.with_memory_space_constraint(value, pltpu.HBM)


def part(value, start, size, axis):
    return lax.dynamic_slice_in_dim(value, start, size, axis)


def encode_call(top, block_list, block_count, x, bias, targets, gain, enc, dec, width):
    tok_rows, model_width = x.shape
    local_latents = enc.shape[1]
    blocks = local_latents // BLOCK
    quad_slots = (blocks + 3) // 4
    rows = tok_rows // 2
    vmem = pl.BlockSpec(memory_space=pltpu.VMEM)
    smem = pl.BlockSpec(memory_space=pltpu.SMEM)
    anyw = pl.BlockSpec(memory_space=pl.ANY)
    return pl.pallas_call(
        functools.partial(encode_decode, top),
        out_shape=(
            pltpu.VMEM((rows, model_width), F32),
            pltpu.VMEM((rows, model_width), BF16),
            pltpu.SMEM((1, blocks + 1), jnp.int32),
            pltpu.VMEM((rows + 16, width), BF16),
            pltpu.VMEM((1, width), F32),
        ),
        in_specs=[anyw, smem] + [anyw] * 6,
        out_specs=(vmem, vmem, smem, vmem, vmem),
        scratch_shapes=[
            pltpu.SMEM(block_list.shape, jnp.int32),
            pltpu.VMEM((tok_rows, model_width), BF16),
            pltpu.VMEM((1, local_latents), F32),
            pltpu.VMEM((rows, model_width), BF16),
            pltpu.VMEM((1, model_width), F32),
            pltpu.VMEM((quad_slots, model_width, 4 * BLOCK), BF16),
            pltpu.VMEM((quad_slots, 4 * BLOCK, model_width), BF16),
            pltpu.VMEM((quad_slots, tok_rows, 4 * BLOCK), BF16),
            pltpu.VMEM((tok_rows, model_width), F32),
            pltpu.SemaphoreType.DMA((5,)),
            pltpu.SemaphoreType.DMA((blocks,)),
            pltpu.SemaphoreType.DMA((blocks,)),
        ],
        compiler_params=pltpu.CompilerParams(vmem_limit_bytes=32 << 20),
        name="encode_decode",
    )(block_list, block_count, x, bias, targets, gain, enc, dec)


def local(residuals, targets, enc_weight, enc_bias, dec_weight, out_gain, block_list, block_count):
    tok_rows, model_width = residuals.shape[1:]
    local_latents = enc_weight.shape[2]
    blocks = local_latents // BLOCK
    slots = (blocks + 3) // 4
    kept = min(KEPT, slots)
    more = max(slots - kept, 1)
    quad = 4 * BLOCK
    layers, latents = lax.axis_size("layer"), lax.axis_size("latent")
    layer, latent = lax.axis_index("layer"), lax.axis_index("latent")
    core = latent % 2
    rows = tok_rows // 2
    chips = latents // 2
    width = model_width // chips
    column = (latent // 2) * width

    layer_bits = [1 << s for s in range((layers - 1).bit_length())]
    chip_bits = [1 << s for s in range((chips - 1).bit_length(), 0, -1)]

    dec_hbm = in_hbm(dec_weight[0])
    vmem = pl.BlockSpec(memory_space=pltpu.VMEM)
    smem = pl.BlockSpec(memory_space=pltpu.SMEM)
    anyw = pl.BlockSpec(memory_space=pl.ANY)
    keep, send, ids, beside, gain = encode_call(
        chip_bits[0], in_hbm(block_list), block_count, in_hbm(residuals[0]), in_hbm(enc_bias), in_hbm(targets[0]), in_hbm(out_gain),
        in_hbm(enc_weight[0]), dec_hbm, width,
    )

    cut = model_width // 2
    got = swap(send, "latent", 1)
    away = (keep[:, :cut] + got[:, :cut].astype(F32)).astype(BF16)
    near_beside = swap(beside, "layer", 1)
    keep, got, away = lax.optimization_barrier((keep, got, away))
    held = keep[:, cut:] + got[:, cut:].astype(F32) + swap(away, "latent", chip_bits[0]).astype(F32)
    for bit in chip_bits[1:]:
        half = held.shape[1] // 2
        upper = (latent & bit) != 0
        away = jnp.where(upper, held[:, :half], held[:, half:]).astype(BF16)
        mine = jnp.where(upper, held[:, half:], held[:, :half])
        held = mine + swap(away, "latent", bit).astype(F32)
    own = held
    sent = own.astype(BF16)
    near = swap(sent, "layer", 1).astype(F32)
    own, sent, near_beside = lax.optimization_barrier((own, sent, near_beside))
    target = beside[:rows]
    near_target = near_beside[:rows]
    near_gain = sum(near_beside[rows + i : rows + i + 1].astype(F32) for i in range(3))
    square = gain * gain
    near_square = near_gain * near_gain
    all_square = square + near_square

    low = (layer & 1) == 0

    def pair_sums(own, near):
        own_error = square * own - gain * target.astype(F32)
        near_error = near_square * near - near_gain * near_target.astype(F32)
        before = jnp.where(low, own, own + near)
        after = jnp.where(low, own_error + near_square * own + near_error, own_error + square * near)
        all_after = own_error + near_error + jnp.where(low, near_square * own, square * near)
        return before, after, own + near, all_after

    before, after, all_before, all_after = pair_sums(own, near)
    after_square = jnp.where(low, square + near_square, square)
    for step in layer_bits[1:]:
        upper = (layer & step) != 0
        there_square = swap(all_square, "layer", step)
        if step == layer_bits[-1]:
            outgoing = jnp.where((layer & step) == 0, all_before, all_after).astype(BF16)
            if len(layer_bits) == 2:
                error_terms = square * own - gain * target.astype(F32) - near_gain * near_target.astype(F32)
                fixed = jnp.where((layer & step) == 0, own, error_terms + jnp.where(low, near_square * own, 0.0))
                factor = jnp.where((layer & step) == 0, 1.0, near_square + jnp.where(low, 0.0, square))
                fixed, factor = lax.optimization_barrier((fixed, factor))
                outgoing = (fixed + factor * near).astype(BF16)
                own, near, outgoing = lax.optimization_barrier((own, near, outgoing))
                before, after, all_before, _ = pair_sums(own, near)
            got = swap(outgoing, "layer", step)
            break
        there_before = swap(all_before.astype(BF16), "layer", step).astype(F32)
        there_after = swap(all_after.astype(BF16), "layer", step).astype(F32)
        before, after = (
            jnp.where(upper, before + there_before, before),
            jnp.where(upper, after + after_square * there_before, after + there_square * all_before + there_after),
        )
        after_square = jnp.where(upper, after_square, after_square + there_square)
        all_before, all_after = (
            all_before + there_before,
            all_after + there_after + jnp.where(upper, all_square * there_before, there_square * all_before),
        )
        all_square = all_square + there_square

    columns = width // 2
    message, stay, send = pl.pallas_call(
        finish,
        out_shape=(
            pltpu.VMEM((rows, width + BLOCK), BF16),
            pltpu.VMEM((rows, columns), BF16),
            pltpu.VMEM((rows, columns), BF16),
        ),
        in_specs=[vmem] * 8,
        out_specs=(vmem, vmem, vmem),
        compiler_params=pltpu.CompilerParams(vmem_limit_bytes=16 << 20),
        name="finish",
    )(got, before, after, all_before, there_square, after_square, gain, beside)

    for bit in reversed(chip_bits[1:]):
        upper = (latent & bit) != 0
        got = swap(message, "latent", bit)
        cut = message.shape[1] - BLOCK
        here, there = message[:, :cut], got[:, :cut]
        squares = (message[:, cut:].astype(F32) + got[:, cut:].astype(F32)).astype(BF16)
        message = jnp.concatenate([jnp.where(upper, there, here), jnp.where(upper, here, there), squares], axis=1)
    top, cut = chip_bits[0], model_width // 2
    got = swap(message, "latent", top)
    near = swap(message[:, :cut], "latent", 1)
    send = jnp.concatenate([send, message[:, cut:]], axis=1)
    near_part, far_kept = pl.pallas_call(
        functools.partial(near_gradient, top),
        out_shape=(pltpu.VMEM((slots, tok_rows, quad), F32), pltpu.VMEM((kept, quad, cut), BF16)),
        in_specs=[smem, vmem, vmem, anyw],
        out_specs=(vmem, vmem),
        scratch_shapes=[
            pltpu.VMEM((tok_rows, cut), BF16),
            pltpu.VMEM((slots, quad, cut), BF16),
            pltpu.SemaphoreType.DMA((blocks,)),
            pltpu.SemaphoreType.DMA((blocks,)),
        ],
        compiler_params=pltpu.CompilerParams(vmem_limit_bytes=24 << 20),
        name="near_gradient",
    )(ids, message, near, dec_hbm)
    got, near_part, send = lax.optimization_barrier((got, near_part, send))
    far = swap(got, "latent", 1)
    other = swap(send, "latent", 1)

    code_grad, recon, loss = pl.pallas_call(
        functools.partial(code_gradient, top),
        out_shape=(
            jax.ShapeDtypeStruct((tok_rows, local_latents), BF16),
            jax.ShapeDtypeStruct((columns, tok_rows), BF16),
            jax.ShapeDtypeStruct((1, 1), F32),
        ),
        in_specs=[smem] + [vmem] * 7 + [anyw],
        out_specs=(vmem, vmem, vmem),
        scratch_shapes=[
            pltpu.VMEM((tok_rows, cut), BF16),
            pltpu.VMEM((tok_rows, columns), F32),
            pltpu.VMEM((more, quad, cut), BF16),
            pltpu.SemaphoreType.DMA((blocks,)),
        ],
        compiler_params=pltpu.CompilerParams(vmem_limit_bytes=16 << 20),
        name="code_gradient",
    )(ids, message, got, far, stay, other, *[pltpu.with_memory_space_constraint(a, pltpu.VMEM) for a in (near_part, far_kept)], dec_hbm)
    return recon.T[None], code_grad[None], loss


def solution(mesh):
    placed = (
        P("layer", "groups", None),
        P("layer", "groups", None),
        P("layer", None, "latent"),
        P("layer", "latent"),
        P("layer", "latent", None),
        P("layer", None),
        P("layer", "groups", None),
        P("layer", "groups"),
    )
    return jax.shard_map(
        local,
        mesh=mesh,
        in_specs=placed,
        out_specs=(
            P("layer", "groups", "latent"),
            P("layer", "groups", "latent"),
            P("groups", "layer"),
        ),
        check_vma=False,
    )
```
